512 devices in a mesh: head: 8 (over z), seq: 64 (over y, x, core).
Axes of the slice: x: 4, y: 8, z: 8, core: 2. Of those that a mesh axis runs over, the one named last changes fastest.
Arguments:
- inputs: bfloat16 [8192, 2048], P('seq', 'head'), may hold values from -6 to 6
- w_query: bfloat16 [2048, 1024], P('seq', 'head'), may hold values from -0.125 to 0.125
- w_key: bfloat16 [2048, 1024], P('seq', 'head'), may hold values from -0.125 to 0.125
- w_value: bfloat16 [2048, 1024], P('seq', 'head'), may hold values from -0.125 to 0.125
- w_beta: bfloat16 [2048, 8], P('seq', 'head'), may hold values from -0.125 to 0.125
- beta_bias: float32 [8], P('head'), may hold values from -1.5 to 1.5
- cotangent: float32 [8192, 1024], P('seq', 'head'), may hold values from -6 to 6
Outputs:
- readout: float32 [8192, 1024], P('seq', 'head')
- grad_query: float32 [2048, 1024], P('seq', 'head')
- grad_key: float32 [2048, 1024], P('seq', 'head')
- grad_value: float32 [2048, 1024], P('seq', 'head')
- grad_beta: float32 [2048, 8], P('seq', 'head')
The draws below stay inside these ranges and needn't reach their ends.
All inputs are finite; a program needn't handle non-finite values.
Results may differ from the reference program's by a relative error of at most 0.00305.
Values may be sent and summed in bfloat16 or wider, within the bound.
A program may use at most 64 MiB of HBM per device.

```python
import math
import jax
import jax.numpy as jnp
from jax import lax

D = 2048
H = 8
DK = 128
BLOCK = 64
TOKENS = 8192


def steps_of(rng, dims, cuts, least, largest):
    loudness, own = 1.0, jax.random.fold_in(rng, 6)
    for axis_at, blocks in cuts:
        heights = jnp.exp(jax.random.uniform(jax.random.fold_in(own, axis_at), (blocks,), jnp.float32, least / len(cuts), largest / len(cuts)))
        loudness = loudness * jnp.repeat(heights, dims[axis_at] // blocks).reshape([-1 if axis == axis_at else 1 for axis in range(len(dims))])
    return loudness


def centred(own_key, shape, deviation, most, cuts=(), held_as=jnp.bfloat16):
    loudness = steps_of(own_key, shape, cuts, -0.22, 0.18) if cuts else 1.0
    entries = jax.random.normal(own_key, shape, jnp.float32) * deviation * loudness
    return jnp.minimum(jnp.maximum(entries, -most), most).astype(held_as)


def setup_inputs(seed: int = 0) -> dict:
    streams_of = jax.random.split(jax.random.key(seed), 8)
    return {
        "inputs": centred(streams_of[0], (TOKENS, D), 1.0, 6.0, ((0, 64), (1, 8))),
        "w_query": centred(streams_of[1], (D, H * DK), D ** -0.5, 0.125, ((0, 64), (1, 8))),
        "w_key": centred(streams_of[2], (D, H * DK), D ** -0.5, 0.125, ((0, 64), (1, 8))),
        "w_value": centred(streams_of[3], (D, H * DK), D ** -0.5, 0.125, ((0, 64), (1, 8))),
        "w_beta": centred(streams_of[4], (D, H), D ** -0.5, 0.125, ((0, 64), (1, 8))),
        "beta_bias": jnp.clip(jax.random.uniform(streams_of[5], (H,), jnp.float32, -1.5, 1.5) * steps_of(streams_of[5], (H,), ((0, 8),), -0.4, 0.0), -1.5, 1.5),
        "cotangent": centred(streams_of[6], (TOKENS, H * DK), 1.0, 6.0, ((0, 64), (1, 8)), jnp.float32),
    }


HIGHEST = lax.Precision.HIGHEST

def unit_rows(raw, head_count):
    rows = raw.reshape(raw.shape[0], head_count, -1)
    scale_sq = lax.optimization_barrier(jnp.mean(rows * rows, axis=-1, keepdims=True)) + 1e-06
    return rows * lax.rsqrt(scale_sq) / math.sqrt(rows.shape[-1])

def blocked(rows):
    return rows.reshape(rows.shape[0] // BLOCK, BLOCK, rows.shape[1], rows.shape[2]).transpose(0, 2, 1, 3)

def wy_factors(key_blk, value_blk, beta_blk):
    key_beta = key_blk * beta_blk[..., None]
    value_beta = value_blk * beta_blk[..., None]
    gram_mat = jnp.einsum('...cd,...ed->...ce', key_beta, key_blk, precision=HIGHEST)
    lower_tri = jnp.tril(gram_mat, -1) + jnp.eye(key_blk.shape[-2], dtype=jnp.float32)
    solved = jax.scipy.linalg.solve_triangular(lower_tri, jnp.concatenate([key_beta, value_beta], axis=-1), lower=True, unit_diagonal=True)
    width = key_blk.shape[-1]
    return (solved[..., :width], solved[..., width:])

def block_step(carry_state, inputs_blk):
    query_blk, key_blk, value_blk, beta_blk = inputs_blk
    w_mat, u_mat = wy_factors(key_blk, value_blk, beta_blk)
    fresh_vals = u_mat - jnp.einsum('hcd,hvd->hcv', w_mat, carry_state, precision=HIGHEST)
    scores = jnp.tril(jnp.einsum('hcd,hed->hce', query_blk, key_blk, precision=HIGHEST))
    readout = jnp.einsum('hcd,hvd->hcv', query_blk, carry_state, precision=HIGHEST) + jnp.einsum('hce,hev->hcv', scores, fresh_vals, precision=HIGHEST)
    new_state = carry_state + jnp.einsum('hcv,hcd->hvd', fresh_vals, key_blk, precision=HIGHEST)
    return (new_state, readout)

def sweep(query_raw, key_raw, value_raw, gate_logit, beta_bias, start_state):
    head_count = beta_bias.shape[0]
    query_all = blocked(unit_rows(query_raw, head_count))
    key_all = blocked(unit_rows(key_raw, head_count))
    value_all = blocked(value_raw.reshape(value_raw.shape[0], head_count, -1))
    beta_rows = 2.0 * jax.nn.sigmoid(gate_logit + beta_bias[None, :])
    beta_all = blocked(beta_rows[..., None])[..., 0]
    end_state, outputs = lax.scan(block_step, start_state, (query_all, key_all, value_all, beta_all))
    readout = outputs.transpose(0, 2, 1, 3).reshape(query_raw.shape[0], -1)
    return (readout, end_state)

def reference(inputs, w_query, w_key, w_value, w_beta, beta_bias, cotangent):
    query_raw = jnp.dot(inputs.astype(jnp.float32), w_query.astype(jnp.float32), preferred_element_type=jnp.float32)
    key_raw = jnp.dot(inputs.astype(jnp.float32), w_key.astype(jnp.float32), preferred_element_type=jnp.float32)
    value_raw = jnp.dot(inputs.astype(jnp.float32), w_value.astype(jnp.float32), preferred_element_type=jnp.float32)
    gate_logit = jnp.dot(inputs.astype(jnp.float32), w_beta.astype(jnp.float32), preferred_element_type=jnp.float32)
    start_state = jnp.zeros((H, DK, DK), jnp.float32)

    def forward(query_in, key_in, value_in, logit_in):
        return sweep(query_in, key_in, value_in, logit_in, beta_bias, start_state)[0]
    readout, pullback = jax.vjp(forward, query_raw, key_raw, value_raw, gate_logit)
    grad_parts = pullback(cotangent)
    results = [jnp.dot(inputs.T.astype(jnp.float32), grad_term.astype(jnp.bfloat16).astype(jnp.float32), preferred_element_type=jnp.float32) for grad_term in grad_parts]
    return (readout, results[0], results[1], results[2], results[3])
```

```python
import functools
import math

import jax
import jax.numpy as jnp
from jax import lax
from jax.experimental import pallas as pl
from jax.experimental.pallas import tpu as pltpu
from jax.sharding import PartitionSpec as P

MESH = pl.DeviceIdType.MESH
F32 = jnp.float32
BF16 = jnp.bfloat16
NN = (((1,), (0,)), ((), ()))
NT = (((1,), (1,)), ((), ()))


def split(a):
    high = a.astype(BF16)
    return high, (a - high.astype(F32)).astype(BF16)


def mm(a, b, form=NN):
    a_high, a_low = split(a)
    b_high, b_low = split(b)
    return mm1(a_high, b_high, form) + (mm1(a_high, b_low, form) + mm1(a_low, b_high, form))


def mm1(a, b, form=NN):
    return lax.dot_general(a, b, form, preferred_element_type=F32)


def kernel(
    nz, ny, nj,
    x_ref, wq_ref, wk_ref, wv_ref, wb_ref, bias_ref, cot_ref,
    o_ref, gq_ref, gk_ref, gv_ref, gb_ref,
    wg, xg, xt, xr, ag, bcs, bcr, gbc, ya, ybc, sgs, sgr, ggs, gg, gbs, gbr, ps, pr, pbs, pbr,
    zs, zr, w1s, w1r, w2s, w2r, w3s, w3r, as_, ar, ass, asr, bs, br, y1s, y1r, y2s, y2r, y3s, y3r,
    xs, xrs, ss, sr, gs, grs, ps_, prs, pbs_, pbrs,
):
    h = lax.axis_index("head")
    s = lax.axis_index("seq")
    y = s // nj
    j = lax.rem(s, nj)
    core = lax.rem(j, 2)
    tok, fb = x_ref.shape
    rw, width = wq_ref.shape
    vp = width // nj

    def zdev(d):
        return (lax.rem(h + d + nz, nz), s)

    def yat(d):
        return lax.rem(y + d + ny, ny)

    def ydev(d):
        return (h, yat(d) * nj + j)

    def jat(d):
        return lax.rem(j + d + nj, nj)

    def jdev(d):
        return (h, y * nj + jat(d))

    sib = j + 1 - 2 * core
    sibdev = (h, y * nj + sib)
    sent = []

    def push(src, dst, ssem, rsem, dev):
        copy = pltpu.make_async_remote_copy(
            src_ref=src, dst_ref=dst, send_sem=ssem, recv_sem=rsem, device_id=dev, device_id_type=MESH
        )
        copy.start()
        sent.append(copy)

    def arrived(dst, ssem, rsem):
        pltpu.make_async_remote_copy(
            src_ref=dst, dst_ref=dst, send_sem=ssem, recv_sem=rsem, device_id=sibdev, device_id_type=MESH
        ).wait_recv()

    barrier = pltpu.get_barrier_semaphore()
    for d in range(1, nz):
        pl.semaphore_signal(barrier, inc=1, device_id=zdev(d), device_id_type=MESH)
    for d in range(1, ny):
        pl.semaphore_signal(barrier, inc=1, device_id=ydev(d), device_id_type=MESH)
    for d in range(1, nj):
        pl.semaphore_signal(barrier, inc=1, device_id=jdev(d), device_id_type=MESH)

    wg[j, y, 0:rw, :] = wq_ref[...]
    wg[j, y, rw:2 * rw, :] = wk_ref[...]
    wg[j, y, 2 * rw:3 * rw, :] = wv_ref[...]
    lane = lax.broadcasted_iota(jnp.int32, (rw, 128), 1)
    row = lax.broadcasted_iota(jnp.int32, (rw, 128), 0)
    put = lane == lax.rem(j * rw, 128) + row
    wb_row = jnp.sum(jnp.where(put, wb_ref[...].astype(F32), 0.0), axis=0, keepdims=True)
    wg[j, y, 3 * rw:3 * rw + 16, :] = jnp.broadcast_to(wb_row, (16, 128)).astype(BF16)
    xg[h] = x_ref[...]

    pl.semaphore_wait(barrier, nz + ny + nj - 3)

    order_z = sorted(range(1, nz), key=lambda d: min(d, nz - d))
    order_y = sorted(range(1, ny), key=lambda d: min(d, ny - d))
    order_j = sorted(range(1, nj), key=lambda d: min(d, nj - d))
    evens = [e for e in order_j if e % 2 == 0]

    for d in order_y:
        push(wg.at[j, y], wg.at[j, y], w1s.at[d], w1r.at[d], ydev(d))
    for n, e in enumerate(evens):
        push(wg.at[j, y], wg.at[j, y], w2s.at[n, 0], w2r.at[n, 0], jdev(e))
    for d in order_z:
        push(xg.at[h], xg.at[h], zs.at[d], zr.at[d], zdev(d))
    for d in order_y:
        part = wg.at[j, yat(-d)]
        arrived(part, w1s.at[d], w1r.at[d])
        for n, e in enumerate(evens):
            push(part, part, w2s.at[n, d], w2r.at[n, d], jdev(e))
    push(wg.at[j], wg.at[j], w3s.at[0], w3r.at[0], sibdev)

    cot = cot_ref[...]
    cot_t = cot.T

    for d in order_z:
        arrived(xg.at[lax.rem(h - d + nz, nz)], zs.at[d], zr.at[d])
    for n, e in enumerate(evens):
        col = wg.at[jat(-e)]
        for d in [0] + order_y:
            arrived(wg.at[jat(-e), yat(-d)], w2s.at[n, d], w2r.at[n, d])
        push(col, col, w3s.at[n + 1], w3r.at[n + 1], sibdev)
    arrived(wg.at[sib], w3s.at[0], w3r.at[0])
    for n, e in enumerate(evens):
        arrived(wg.at[lax.rem(sib - e + nj, nj)], w3s.at[n + 1], w3r.at[n + 1])

    raw = jnp.zeros((tok, 3 * width), F32)
    lacc = jnp.zeros((tok, 128), F32)
    per = 128 // rw
    for b in range(nz):
        xb = xg[b]
        w_b = jnp.concatenate(
            [wg[:, b, m * rw:(m + 1) * rw, :].reshape(fb, width) for m in range(3)], axis=1
        )
        raw = raw + mm1(xb, w_b)
        for g in range(fb // 128):
            w_row = jnp.sum(wg[g * per:(g + 1) * per, b, 3 * rw:3 * rw + 16, :].astype(F32), axis=0)[:1]
            lacc = lacc + xb[:, g * 128:(g + 1) * 128].astype(F32) * w_row
    logit = jnp.sum(lacc, axis=1, keepdims=True) + bias_ref[0]
    beta = 2.0 * jax.nn.sigmoid(logit)

    def unit(r):
        scale = lax.rsqrt(jnp.mean(r * r, axis=1, keepdims=True) + 1e-06) * (1.0 / math.sqrt(width))
        return r * scale, scale

    q, q_scale = unit(raw[:, :width])
    k, k_scale = unit(raw[:, width:2 * width])
    v = raw[:, 2 * width:]

    ri = lax.broadcasted_iota(jnp.int32, (tok, tok), 0)
    ci = lax.broadcasted_iota(jnp.int32, (tok, tok), 1)
    lower = ri > ci
    upper = ri < ci
    lower_d = ri >= ci
    upper_d = ri <= ci
    eye = jnp.where(ri == ci, 1.0, 0.0).astype(F32)

    gram = mm(k, k, NT)
    low = jnp.where(lower, beta * gram, 0.0)
    t_mat = eye - jnp.where((ri // 2) == (ci // 2), low, 0.0)
    size = 2
    while size < tok:
        level = ((ri // (2 * size)) == (ci // (2 * size))) & ((ri // size) != (ci // size))
        t_mat = t_mat - mm(t_mat, mm(jnp.where(level, low, 0.0), t_mat))
        size *= 2
    wu = mm(t_mat, jnp.concatenate([beta * k, beta * v], axis=1))
    w_mat, u_mat = wu[:, :width], wu[:, width:]
    m_mat = jnp.where(lower_d, mm(q, k, NT), 0.0)
    mwu = mm(m_mat, wu)
    q_eff = q - mwu[:, :width]
    m_u = mwu[:, width:]
    kwu = mm(k.T, wu)
    ag[j] = eye - kwu[:, :width]
    bcs[:, 0] = kwu[:, width:].T.reshape(nj, vp, width)
    bcs[:, 1] = mm(cot_t, q_eff).reshape(nj, vp, width)
    bcr[j] = bcs[j]

    push(ag.at[j], ag.at[j], ass.at[0], asr.at[0], sibdev)
    for n, e in enumerate(evens):
        push(ag.at[j], ag.at[j], as_.at[n], ar.at[n], jdev(e))
    for d in order_j:
        push(bcs.at[jat(d)], bcr.at[j], bs.at[d], br.at[d], jdev(d))

    m_t = jnp.where(upper_d, mm(k, q, NT), 0.0)
    ty = mm(t_mat.T, jnp.concatenate([k, mm(m_t, cot)], axis=1))
    t_k, y_0 = ty[:, :width], ty[:, width:]
    for b in range(nz):
        xt[:, b * rw:(b + 1) * rw, :] = xg[b].astype(F32).T.astype(BF16).reshape(nj, rw, tok)

    for n, e in enumerate(evens):
        part = ag.at[jat(-e)]
        arrived(part, as_.at[n], ar.at[n])
        push(part, part, ass.at[n + 1], asr.at[n + 1], sibdev)
    arrived(ag.at[sib], ass.at[0], asr.at[0])
    for n, e in enumerate(evens):
        arrived(ag.at[lax.rem(sib - e + nj, nj)], ass.at[n + 1], asr.at[n + 1])
    for d in order_j:
        arrived(bcr.at[jat(-d)], bs.at[d], br.at[d])

    p_mat = ag[0]
    b_row = bcr[0, 0]
    c_row = bcr[nj - 1, 1]
    befores = [None, p_mat]
    b_before = [None, b_row]
    c_after = {nj - 2: c_row}
    for i in range(1, nj):
        p_mat = mm(ag[i], p_mat)
        b_row = mm(b_row, ag[i], NT) + bcr[i, 0]
        c_row = mm(c_row, ag[nj - 1 - i]) + bcr[nj - 1 - i, 1]
        befores.append(p_mat)
        b_before.append(b_row)
        c_after[nj - 2 - i] = c_row
    ybc[y] = jnp.zeros((vp, width), F32)
    gbc[0] = b_row
    gbc[1] = c_row
    half = tok // 2
    top, bottom = p_mat[:half].astype(BF16), p_mat[half:].astype(BF16)
    ya[core, y] = jnp.where(core == 0, top, bottom)
    for d in order_y:
        push(ya.at[core, y], ya.at[core, y], y1s.at[d], y1r.at[d], ydev(d))
        side = (y + d) // ny
        push(gbc.at[side], ybc.at[y], y2s.at[d], y2r.at[d], ydev(d))
    for d in order_j:
        xr_dst = xr.at[j]
        push(xt.at[jat(d)], xr_dst, xs.at[d], xrs.at[d], jdev(d))
    xr[j] = xt[j]

    afters = {nj - 2: ag[nj - 1]}
    for i in range(nj - 3, -1, -1):
        afters[i] = mm(afters[i + 1], ag[i + 1])

    for d in order_y:
        arrived(ya.at[core, yat(-d)], y1s.at[d], y1r.at[d])
    push(ya.at[core], ya.at[core], y3s, y3r, sibdev)
    for d in order_y:
        arrived(ybc.at[yat(-d)], y2s.at[d], y2r.at[d])
    arrived(ya.at[1 - core], y3s, y3r)

    def full(t):
        return jnp.concatenate([ya[0, t], ya[1, t]], axis=0).astype(F32)

    s_g = jnp.zeros((vp, width), F32)
    g_g = jnp.zeros((vp, width), F32)
    for t in range(ny - 1):
        s_g = jnp.where(t < y, mm(s_g, full(t), NT) + ybc[t], s_g)
        u = ny - 1 - t
        g_g = jnp.where(u > y, mm(g_g, full(u)) + ybc[u], g_g)

    sgs[0, 0] = s_g
    sgs[nj - 1, 1] = g_g
    for i in range(1, nj):
        sgs[i, 0] = mm(s_g, befores[i], NT) + b_before[i]
    for i in range(nj - 1):
        sgs[i, 1] = mm(g_g, afters[i]) + c_after[i]
    for d in order_j:
        push(sgs.at[jat(d)], sgr.at[j], ss.at[d], sr.at[d], jdev(d))
    sgr[j] = sgs[j]
    for d in order_j:
        arrived(sgr.at[jat(-d)], ss.at[d], sr.at[d])

    state = sgr[:, 0].reshape(width, width)
    grad = sgr[:, 1].reshape(width, width)
    y_mat = y_0 + mm(t_k, grad, NT)
    b_y = beta * y_mat
    ggs[2] = b_y.astype(BF16)

    def share(m):
        for d in order_j:
            push(ggs.at[m], gg.at[j, m], gs.at[m, d], grs.at[m, d], jdev(d))
        gg[j, m] = ggs[m]

    share(2)
    fresh = u_mat - mm(w_mat, state, NT)
    o_ref[...] = mm(q_eff, state, NT) + m_u
    d_m = jnp.where(lower_d, mm(cot, fresh, NT), 0.0)
    d_q = mm(cot, state) + mm(d_m, k)
    ggs[0] = (q_scale * (d_q - q * jnp.sum(d_q * q, axis=1, keepdims=True))).astype(BF16)
    share(0)
    rest = v - mm(k, state, NT)
    d_mt = jnp.where(upper_d, mm(fresh, cot, NT), 0.0)
    yd = jnp.where(lower, mm(y_mat, fresh, NT), 0.0)
    both = beta * yd + jnp.where(upper, mm(fresh, b_y, NT), 0.0)
    d_k = mm(fresh, grad) - mm(b_y, state) + mm(d_mt, q) - mm(both, k)
    ggs[1] = (k_scale * (d_k - k * jnp.sum(d_k * k, axis=1, keepdims=True))).astype(BF16)
    share(1)
    d_beta = jnp.sum(y_mat * rest - yd * gram, axis=1, keepdims=True)
    d_logit = d_beta * beta * (1.0 - 0.5 * beta)
    dl_row = jnp.sum(eye * d_logit, axis=0, keepdims=True)
    gbs[...] = jnp.broadcast_to(dl_row, (16, tok)).astype(BF16)
    for d in order_j:
        push(gbs, gbr.at[j], gs.at[3, d], grs.at[3, d], jdev(d))
    gbr[j] = gbs[...]

    for d in order_j:
        arrived(xr.at[jat(-d)], xs.at[d], xrs.at[d])
    x_t = jnp.concatenate([xr[i] for i in range(nj)], axis=1)

    outs = {0: gq_ref, 1: gk_ref, 2: gv_ref}
    for m in (2, 0, 1):
        for d in order_j:
            arrived(gg.at[jat(-d), m], gs.at[m, d], grs.at[m, d])
        part = mm1(x_t, gg[:, m].reshape(nj * tok, width)).reshape(ny, rw, width)
        pr[m, y] = jnp.zeros((rw, width), BF16)
        ps[m] = part.astype(BF16)
        for d in order_y:
            push(ps.at[m, yat(d)], pr.at[m, y], ps_.at[m, d], prs.at[m, d], ydev(d))
        for t in range(ny):
            @pl.when(t == y)
            def _():
                outs[m][...] = part[t]
    for d in order_j:
        arrived(gbr.at[jat(-d)], gs.at[3, d], grs.at[3, d])
    pb = mm1(jnp.concatenate([gbr[i] for i in range(nj)], axis=1), x_t, NT)
    for g in range(fb // 128):
        pbs[g] = pb[:8, g * 128:(g + 1) * 128]
    for d in order_y:
        push(pbs.at[yat(d) * rw // 128], pbr.at[y], pbs_.at[d], pbrs.at[d], ydev(d))
    pbr[y] = pbs[y * rw // 128]

    for m in (2, 0, 1):
        for d in order_y:
            arrived(pr.at[m, yat(-d)], ps_.at[m, d], prs.at[m, d])
        outs[m][...] += jnp.sum(pr[m].astype(F32), axis=0)
    for d in order_y:
        arrived(pbr.at[yat(-d)], pbs_.at[d], pbrs.at[d])
    pb_row = jnp.sum(pbr[...], axis=0)[:1]
    take = lane == lax.rem(y * rw, 128) + row
    gb_ref[...] = jnp.sum(jnp.where(take, pb_row, 0.0), axis=1, keepdims=True)

    for copy in sent:
        copy.wait_send()


def per_device(mesh, *args):
    inputs, w_query, w_key, w_value, w_beta, beta_bias, cotangent = args
    nz = mesh.shape["head"]
    ny = nz
    nj = mesh.shape["seq"] // ny
    tok, fb = inputs.shape
    rw, width = w_query.shape
    vp = width // nj
    ne = nj // 2
    vmem = pl.BlockSpec(memory_space=pltpu.VMEM)
    dma = pltpu.SemaphoreType.DMA
    scratch = [
        pltpu.VMEM((nj, ny, 3 * rw + 16, 128), BF16),
        pltpu.VMEM((nz, tok, fb), BF16),
        pltpu.VMEM((nj, nz * rw, tok), BF16),
        pltpu.VMEM((nj, nz * rw, tok), BF16),
        pltpu.VMEM((nj, width, width), F32),
        pltpu.VMEM((nj, 2, vp, width), F32),
        pltpu.VMEM((nj, 2, vp, width), F32),
        pltpu.VMEM((2, vp, width), F32),
        pltpu.VMEM((2, ny, width // 2, width), BF16),
        pltpu.VMEM((ny, vp, width), F32),
        pltpu.VMEM((nj, 2, vp, width), F32),
        pltpu.VMEM((nj, 2, vp, width), F32),
        pltpu.VMEM((3, tok, width), BF16),
        pltpu.VMEM((nj, 3, tok, width), BF16),
        pltpu.VMEM((16, tok), BF16),
        pltpu.VMEM((nj, 16, tok), BF16),
        pltpu.VMEM((3, ny, rw, width), BF16),
        pltpu.VMEM((3, ny, rw, width), BF16),
        pltpu.VMEM((fb // 128, 8, 128), F32),
        pltpu.VMEM((ny, 8, 128), F32),
        dma((nz,)), dma((nz,)),
        dma((ny,)), dma((ny,)),
        dma((ne, ny)), dma((ne, ny)),
        dma((ne,)), dma((ne,)),
        dma((ne,)), dma((ne,)),
        dma((ne,)), dma((ne,)),
        dma((nj,)), dma((nj,)),
        dma((ny,)), dma((ny,)),
        dma((ny,)), dma((ny,)),
        dma, dma,
        dma((nj,)), dma((nj,)),
        dma((nj,)), dma((nj,)),
        dma((4, nj)), dma((4, nj)),
        dma((3, ny)), dma((3, ny)),
        dma((ny,)), dma((ny,)),
    ]
    return pl.pallas_call(
        functools.partial(kernel, nz, ny, nj),
        out_shape=(
            jax.ShapeDtypeStruct((tok, width), F32),
            jax.ShapeDtypeStruct((rw, width), F32),
            jax.ShapeDtypeStruct((rw, width), F32),
            jax.ShapeDtypeStruct((rw, width), F32),
            jax.ShapeDtypeStruct((rw, 1), F32),
        ),
        in_specs=[vmem, vmem, vmem, vmem, vmem, pl.BlockSpec(memory_space=pltpu.SMEM), vmem],
        out_specs=(vmem,) * 5,
        scratch_shapes=scratch,
        compiler_params=pltpu.CompilerParams(
            collective_id=0, has_side_effects=True, vmem_limit_bytes=48 * 1024 * 1024
        ),
        name="delta_step",
    )(inputs, w_query, w_key, w_value, w_beta, beta_bias, cotangent)


def solution(mesh):
    return jax.shard_map(
        functools.partial(per_device, mesh),
        mesh=mesh,
        in_specs=(P("seq", "head"),) * 5 + (P("head"), P("seq", "head")),
        out_specs=(P("seq", "head"),) * 5,
        check_vma=False,
    )
```

```python
import functools
import math

import jax
import jax.numpy as jnp
from jax import lax
from jax.experimental import pallas as pl
from jax.experimental.pallas import tpu as pltpu
from jax.sharding import PartitionSpec as P

MESH = pl.DeviceIdType.MESH
F32 = jnp.float32
BF16 = jnp.bfloat16
NN = (((1,), (0,)), ((), ()))
NT = (((1,), (1,)), ((), ()))


def split(a):
    high = a.astype(BF16)
    return high, (a - high.astype(F32)).astype(BF16)


def mm(a, b, form=NN):
    a_high, a_low = split(a)
    b_high, b_low = split(b)
    return mm1(a_high, b_high, form) + (mm1(a_high, b_low, form) + mm1(a_low, b_high, form))


def mm1(a, b, form=NN):
    return lax.dot_general(a, b, form, preferred_element_type=F32)


def kernel(
    nz, ny, nj,
    x_ref, wq_ref, wk_ref, wv_ref, wb_ref, bias_ref, cot_ref,
    o_out, gq_out, gk_out, gv_out, gb_out,
    o_ref, gq_ref, gk_ref, gv_ref, gb_ref, cotv, wbv, wg, wb1, wb2, xg, xt, xr, ag, bcs, bcr, gbc, ya, ybc, sgs, sgr, ggs, gg, gbs, gbr, ps, pr, pbs, pbr,
    ls, zs, zr, w1s, w1r, w2s, w2r, w3s, w3r, v1s, v1r, v2s, v2r, v3s, v3r, as_, ar, ass, asr, bs, br, y1s, y1r, y2s, y2r, y3s, y3r,
    xs, xrs, ss, sr, gs, grs, hs, hr, ps_, prs, pbs_, pbrs,
):
    h = lax.axis_index("head")
    s = lax.axis_index("seq")
    y = s // nj
    j = lax.rem(s, nj)
    core = lax.rem(j, 2)
    tok, fb = x_ref.shape
    rw, width = wq_ref.shape
    vp = width // nj

    def zdev(d):
        return (lax.rem(h + d + nz, nz), s)

    def yat(d):
        return lax.rem(y + d + ny, ny)

    def ydev(d):
        return (h, yat(d) * nj + j)

    def jat(d):
        return lax.rem(j + d + nj, nj)

    def jdev(d):
        return (h, y * nj + jat(d))

    sib = j + 1 - 2 * core
    sibdev = (h, y * nj + sib)
    sent = []

    def drain():
        for copy in sent:
            copy.wait_send()
        del sent[:]

    def push(src, dst, sems, at, dev):
        copy = pltpu.make_async_remote_copy(
            src_ref=src, dst_ref=dst, send_sem=sems[0].at[at], recv_sem=sems[1].at[at], device_id=dev, device_id_type=MESH
        )
        copy.start()
        sent.append(copy)

    def arrived(dst, sems, at):
        pltpu.make_async_remote_copy(
            src_ref=dst, dst_ref=dst, send_sem=sems[0].at[at], recv_sem=sems[1].at[at], device_id=sibdev, device_id_type=MESH
        ).wait_recv()

    local = [
        pltpu.make_async_copy(x_ref, xg.at[h], ls.at[0]),
        pltpu.make_async_copy(wq_ref, wg.at[j, y, pl.ds(0, rw)], ls.at[1]),
        pltpu.make_async_copy(wk_ref, wg.at[j, y, pl.ds(rw, rw)], ls.at[2]),
        pltpu.make_async_copy(wv_ref, wg.at[j, y, pl.ds(2 * rw, rw)], ls.at[3]),
        pltpu.make_async_copy(cot_ref, cotv, ls.at[4]),
        pltpu.make_async_copy(wb_ref, wbv, ls.at[10]),
    ]
    for copy in local:
        copy.start()

    barrier = pltpu.get_barrier_semaphore()
    for d in (1, nz - 1, 2, nz - 2):
        pl.semaphore_signal(barrier, inc=1, device_id=zdev(d), device_id_type=MESH)
    for d in range(1, ny):
        pl.semaphore_signal(barrier, inc=1, device_id=ydev(d), device_id_type=MESH)
    for d in range(1, nj):
        pl.semaphore_signal(barrier, inc=1, device_id=jdev(d), device_id_type=MESH)

    per = 128 // rw
    lane = lax.broadcasted_iota(jnp.int32, (1, 128), 1)
    for copy in local:
        copy.wait()
    wb_row = jnp.concatenate([wbv[...].astype(F32)] * per, axis=1)
    wb_row = jnp.where(lane // rw == lax.rem(j, per), wb_row, 0.0)
    wb1[y] = jnp.broadcast_to(wb_row, (16, 128)).astype(BF16)

    pl.semaphore_wait(barrier, ny + nj + 2)

    order_y = sorted(range(1, ny), key=lambda d: min(d, ny - d))
    order_j = sorted(range(1, nj), key=lambda d: min(d, nj - d))
    evens = [e for e in order_j if e % 2 == 0]

    for d in order_y:
        push(wg.at[j, y], wg.at[j, y], (w1s, w1r), (d,), ydev(d))
    for n, e in enumerate(evens):
        push(wg.at[j, y], wg.at[j, y], (w2s, w2r), (n, 0), jdev(e))
    for d in (2, nz - 2, 1, nz - 1):
        push(xg.at[h], xg.at[h], (zs, zr), (d,), zdev(d))
    for d in order_y:
        push(wb1.at[y], wb1.at[y], (v1s, v1r), (d,), ydev(d))
    push(wg.at[j, y], wg.at[j, y], (w3s, w3r), (0, 0), sibdev)

    def take_w(d):
        part = wg.at[j, yat(-d)]
        arrived(part, (w1s, w1r), (d,))
        for n, e in enumerate(evens):
            push(part, part, (w2s, w2r), (n, d), jdev(e))
        push(part, part, (w3s, w3r), (0, d), sibdev)

    for d in order_y[:4]:
        take_w(d)
    up, down = lax.rem(h - 2 + nz, nz), lax.rem(h + 2, nz)
    mid = tok // 2
    arrived(xg.at[up], (zs, zr), (2,))
    push(xg.at[up], xg.at[up], (zs, zr), (3,), zdev(1))
    push(xg.at[up, pl.ds(0, mid)], xg.at[up, pl.ds(0, mid)], (zs, zr), (4,), zdev(2))
    arrived(xg.at[down], (zs, zr), (nz - 2,))
    push(xg.at[down], xg.at[down], (zs, zr), (nz - 3,), zdev(-1))
    push(xg.at[down, pl.ds(mid, mid)], xg.at[down, pl.ds(mid, mid)], (zs, zr), (0,), zdev(-2))
    for d in order_y[4:]:
        take_w(d)
    for d in order_y:
        arrived(wb1.at[yat(-d)], (v1s, v1r), (d,))
    turn = lax.broadcasted_iota(jnp.int32, (16, 128), 0)
    col = jnp.zeros((16, 128), F32)
    for b in range(ny):
        col = jnp.where(turn == b, wb1[b].astype(F32), col)
    wb2[j] = col.astype(BF16)
    push(wb2.at[j], wb2.at[j], (v3s, v3r), (0,), sibdev)
    for n, e in enumerate(evens):
        push(wb2.at[j], wb2.at[j], (v2s, v2r), (n,), jdev(e))

    cot = cotv[...]
    cot_t = cot.T

    for d in [0] + order_y:
        for n, e in enumerate(evens):
            part = wg.at[jat(-e), yat(-d)]
            arrived(part, (w2s, w2r), (n, d))
            push(part, part, (w3s, w3r), (n + 1, d), sibdev)
    for n, e in enumerate(evens):
        part = wb2.at[jat(-e)]
        arrived(part, (v2s, v2r), (n,))
        push(part, part, (v3s, v3r), (n + 1,), sibdev)
    for d in (1, nz - 1, 3, nz - 3):
        arrived(xg.at[lax.rem(h - d + nz, nz)], (zs, zr), (d,))
    far = lax.rem(h + 4, nz)
    arrived(xg.at[far, pl.ds(0, mid)], (zs, zr), (4,))
    arrived(xg.at[far, pl.ds(mid, mid)], (zs, zr), (0,))
    for n, e in enumerate([0] + evens):
        part = lax.rem(sib - e + nj, nj)
        for d in [0] + order_y:
            arrived(wg.at[part, yat(-d)], (w3s, w3r), (n, d))
        arrived(wb2.at[part], (v3s, v3r), (n,))

    raw = jnp.zeros((tok, 3 * width), F32)
    lacc = jnp.zeros((tok, 128), F32)
    w_rows = [
        jnp.sum(wb2[g * per:(g + 1) * per].astype(F32), axis=0) for g in range(fb // 128)
    ]
    for b in range(nz):
        xb = xg[b]
        w_b = jnp.concatenate(
            [wg[:, b, m * rw:(m + 1) * rw, :].reshape(fb, width) for m in range(3)], axis=1
        )
        raw = raw + mm1(xb, w_b)
        for g in range(fb // 128):
            w_row = w_rows[g][b:b + 1]
            lacc = lacc + xb[:, g * 128:(g + 1) * 128].astype(F32) * w_row
    logit = jnp.sum(lacc, axis=1, keepdims=True) + bias_ref[0]
    beta = 2.0 * jax.nn.sigmoid(logit)

    def unit(r):
        scale = lax.rsqrt(jnp.mean(r * r, axis=1, keepdims=True) + 1e-06) * (1.0 / math.sqrt(width))
        return r * scale, scale

    q, q_scale = unit(raw[:, :width])
    k, k_scale = unit(raw[:, width:2 * width])
    v = raw[:, 2 * width:]

    ri = lax.broadcasted_iota(jnp.int32, (tok, tok), 0)
    ci = lax.broadcasted_iota(jnp.int32, (tok, tok), 1)
    lower = ri > ci
    upper = ri < ci
    lower_d = ri >= ci
    upper_d = ri <= ci
    eye = jnp.where(ri == ci, 1.0, 0.0).astype(F32)

    gram = mm(k, k, NT)
    low = jnp.where(lower, beta * gram, 0.0)
    t_mat = eye - jnp.where((ri // 2) == (ci // 2), low, 0.0)
    size = 2
    while size < tok:
        level = ((ri // (2 * size)) == (ci // (2 * size))) & ((ri // size) != (ci // size))
        t_mat = t_mat - mm(t_mat, mm(jnp.where(level, low, 0.0), t_mat))
        size *= 2
    k_t = k.T
    w_mat = mm(t_mat, beta * k)
    ag[j] = eye - mm(k_t, w_mat)
    push(ag.at[j], ag.at[j], (ass, asr), (0,), sibdev)
    for n, e in enumerate(evens):
        push(ag.at[j], ag.at[j], (as_, ar), (n,), jdev(e))
    m_mat = jnp.where(lower_d, mm(q, k, NT), 0.0)
    q_eff = q - mm(m_mat, w_mat)
    u_mat = mm(t_mat, beta * v)
    bcs[:, 0] = mm(k_t, u_mat).T.reshape(nj, vp, width)
    bcs[:, 1] = mm(cot_t, q_eff).reshape(nj, vp, width)
    bcr[j] = bcs[j]
    for d in order_j:
        push(bcs.at[jat(d)], bcr.at[j], (bs, br), (d,), jdev(d))

    m_t = jnp.where(upper_d, mm(k, q, NT), 0.0)
    ty = mm(t_mat.T, jnp.concatenate([k, mm(m_t, cot)], axis=1))
    t_k, y_0 = ty[:, :width], ty[:, width:]
    m_u = mm(m_mat, u_mat)
    for b in range(nz):
        xt[:, b * rw:(b + 1) * rw, :] = xg[b].astype(F32).T.astype(BF16).reshape(nj, rw, tok)

    drain()
    for n, e in enumerate(evens):
        part = ag.at[jat(-e)]
        arrived(part, (as_, ar), (n,))
        push(part, part, (ass, asr), (n + 1,), sibdev)
    arrived(ag.at[sib], (ass, asr), (0,))
    for n, e in enumerate(evens):
        arrived(ag.at[lax.rem(sib - e + nj, nj)], (ass, asr), (n + 1,))
    for d in order_j:
        arrived(bcr.at[jat(-d)], (bs, br), (d,))

    pair_p, pair_b, pair_c = [], [], []
    for i in range(0, nj, 2):
        pair_p.append(mm(ag[i + 1], ag[i]))
        pair_b.append(mm(bcr[i, 0], ag[i + 1], NT) + bcr[i + 1, 0])
        pair_c.append(mm(bcr[i + 1, 1], ag[i]) + bcr[i, 1])
    p_mat, b_row, c_row = pair_p[0], pair_b[0], pair_c[-1]
    befores = [None, ag[0], p_mat]
    b_before = [None, bcr[0, 0], b_row]
    c_after = {nj - 2: bcr[nj - 1, 1], nj - 3: c_row}
    for i in range(1, nj // 2):
        back = nj // 2 - 1 - i
        p_mat = mm(pair_p[i], p_mat)
        b_row = mm(b_row, pair_p[i], NT) + pair_b[i]
        c_row = mm(c_row, pair_p[back]) + pair_c[back]
        befores += [None, p_mat]
        b_before += [None, b_row]
        c_after[2 * back - 1] = c_row
    ybc[y] = jnp.zeros((vp, width), F32)
    gbc[0] = b_row
    gbc[1] = c_row
    half = tok // 2
    top, bottom = p_mat[:half].astype(BF16), p_mat[half:].astype(BF16)
    ya[core, y] = jnp.where(core == 0, top, bottom)
    for d in order_y:
        push(ya.at[core, y], ya.at[core, y], (y1s, y1r), (d,), ydev(d))
        side = (y + d) // ny
        push(gbc.at[side], ybc.at[y], (y2s, y2r), (d,), ydev(d))
    for d in order_j:
        xr_dst = xr.at[j]
        push(xt.at[jat(d)], xr_dst, (xs, xrs), (d,), jdev(d))
    xr[j] = xt[j]

    afters = {nj - 2: ag[nj - 1], nj - 3: pair_p[-1]}
    for i in range(nj // 2 - 2, -1, -1):
        afters[2 * i - 1] = mm(afters[2 * i + 1], pair_p[i])
        afters[2 * i] = mm(afters[2 * i + 1], ag[2 * i + 1])
        c_after[2 * i] = mm(c_after[2 * i + 1], ag[2 * i + 1]) + bcr[2 * i + 1, 1]
        m = nj - 2 - 2 * i
        befores[m + 1] = mm(ag[m], befores[m])
        b_before[m + 1] = mm(b_before[m], ag[m], NT) + bcr[m, 0]
    drain()
    for d in order_y:
        arrived(ya.at[core, yat(-d)], (y1s, y1r), (d,))
    push(ya.at[core], ya.at[core], (y3s, y3r), (0,), sibdev)
    for d in order_y:
        arrived(ybc.at[yat(-d)], (y2s, y2r), (d,))
    arrived(ya.at[1 - core], (y3s, y3r), (0,))

    def full(t):
        return jnp.concatenate([ya[0, t], ya[1, t]], axis=0).astype(F32)

    s_g = jnp.zeros((vp, width), F32)
    g_g = jnp.zeros((vp, width), F32)
    for t in range(ny - 1):
        s_g = jnp.where(t < y, mm(s_g, full(t), NT) + ybc[t], s_g)
        u = ny - 1 - t
        g_g = jnp.where(u > y, mm(g_g, full(u)) + ybc[u], g_g)

    sgs[0, 0] = s_g
    sgs[nj - 1, 1] = g_g
    for i in range(1, nj):
        sgs[i, 0] = mm(s_g, befores[i], NT) + b_before[i]
    for i in range(nj - 1):
        sgs[i, 1] = mm(g_g, afters[i]) + c_after[i]
    for d in order_j:
        push(sgs.at[jat(d)], sgr.at[j], (ss, sr), (d,), jdev(d))
    sgr[j] = sgs[j]
    drain()
    for d in order_j:
        arrived(sgr.at[jat(-d)], (ss, sr), (d,))

    state = sgr[:, 0].reshape(width, width)
    grad = sgr[:, 1].reshape(width, width)
    y_mat = y_0 + mm(t_k, grad, NT)
    b_y = beta * y_mat
    ggs[2] = b_y.astype(BF16)

    def share(src, dst, m):
        push(src, dst, (hs, hr), (m, 0), sibdev)
        for n, e in enumerate(evens):
            push(src, dst, (gs, grs), (m, n), jdev(e))

    def shared(at, m):
        for n, e in enumerate(evens):
            part = at(jat(-e))
            arrived(part, (gs, grs), (m, n))
            push(part, part, (hs, hr), (m, n + 1), sibdev)

    def collected(at, m):
        for n, e in enumerate([0] + evens):
            arrived(at(lax.rem(sib - e + nj, nj)), (hs, hr), (m, n))

    gg[j, 2] = ggs[2]
    share(ggs.at[2], gg.at[j, 2], 2)
    fresh = u_mat - mm(w_mat, state, NT)
    o_ref[...] = mm(q_eff, state, NT) + m_u
    stores = [pltpu.make_async_copy(o_ref, o_out, ls.at[5])]
    stores[0].start()
    d_m = jnp.where(lower_d, mm(cot, fresh, NT), 0.0)
    d_q = mm(cot, state) + mm(d_m, k)
    ggs[0] = (q_scale * (d_q - q * jnp.sum(d_q * q, axis=1, keepdims=True))).astype(BF16)
    gg[j, 0] = ggs[0]
    share(ggs.at[0], gg.at[j, 0], 0)
    rest = v - mm(k, state, NT)
    d_mt = jnp.where(upper_d, mm(fresh, cot, NT), 0.0)
    yd = jnp.where(lower, mm(y_mat, fresh, NT), 0.0)
    both = beta * yd + jnp.where(upper, mm(fresh, b_y, NT), 0.0)
    d_k = mm(fresh, grad) - mm(b_y, state) + mm(d_mt, q) - mm(both, k)
    ggs[1] = (k_scale * (d_k - k * jnp.sum(d_k * k, axis=1, keepdims=True))).astype(BF16)
    gg[j, 1] = ggs[1]
    share(ggs.at[1], gg.at[j, 1], 1)
    d_beta = jnp.sum(y_mat * rest - yd * gram, axis=1, keepdims=True)
    d_logit = d_beta * beta * (1.0 - 0.5 * beta)
    dl_row = jnp.sum(eye * d_logit, axis=0, keepdims=True)
    gbs[...] = jnp.broadcast_to(dl_row, (16, tok)).astype(BF16)
    gbr[j] = gbs[...]
    share(gbs, gbr.at[j], 3)

    for d in order_j:
        arrived(xr.at[jat(-d)], (xs, xrs), (d,))
    x_t = jnp.concatenate([xr[i] for i in range(nj)], axis=1)

    outs = {0: gq_ref, 1: gk_ref, 2: gv_ref}
    places = [
        lambda i: gg.at[i, 0],
        lambda i: gg.at[i, 1],
        lambda i: gg.at[i, 2],
        lambda i: gbr.at[i],
    ]
    def spread(m):
        collected(places[m], m)
        part = mm1(x_t, gg[:, m].reshape(nj * tok, width)).reshape(ny, rw, width)
        pr[m, y] = jnp.zeros((rw, width), BF16)
        ps[m] = part.astype(BF16)
        for d in order_y:
            push(ps.at[m, yat(d)], pr.at[m, y], (ps_, prs), (m, d), ydev(d))
        own = part[0]
        for t in range(1, ny):
            own = jnp.where(t == y, part[t], own)
        outs[m][...] = own

    for m in (2, 0, 1, 3):
        shared(places[m], m)
    for m in (2, 0, 1):
        spread(m)
    collected(places[3], 3)
    pb = mm1(jnp.concatenate([gbr[i] for i in range(nj)], axis=1), x_t, NT)
    for g in range(fb // 128):
        pbs[g] = pb[:8, g * 128:(g + 1) * 128]
    for d in order_y:
        push(pbs.at[yat(d) * rw // 128], pbr.at[y], (pbs_, pbrs), (d,), ydev(d))
    pbr[y] = pbs[y * rw // 128]

    def store(src, dst, at):
        stores.append(pltpu.make_async_copy(src, dst, ls.at[at]))
        stores[-1].start()

    out_refs = {0: gq_out, 1: gk_out, 2: gv_out}
    for m in (2, 0, 1):
        for d in order_y:
            arrived(pr.at[m, yat(-d)], (ps_, prs), (m, d))
        outs[m][...] += jnp.sum(pr[m].astype(F32), axis=0)
        store(outs[m], out_refs[m], 6 + m)
    for d in order_y:
        arrived(pbr.at[yat(-d)], (pbs_, pbrs), (d,))
    pb_row = jnp.sum(pbr[...], axis=0)[:1]
    gb_row = jnp.zeros((1, rw), F32)
    for g in range(per):
        gb_row = jnp.where(lax.rem(y, per) == g, pb_row[:, g * rw:(g + 1) * rw], gb_row)
    gb_ref[...] = gb_row
    store(gb_ref, gb_out, 9)

    drain()
    for copy in stores:
        copy.wait()


def write_out(o_in, gq_in, gk_in, gv_in, gb_in, o_out, gq_out, gk_out, gv_out, gb_out, sems):
    pairs = [(o_in, o_out), (gq_in, gq_out), (gk_in, gk_out), (gv_in, gv_out), (gb_in, gb_out)]
    copies = [pltpu.make_async_copy(pairs[i][0], pairs[i][1], sems.at[i]) for i in range(5)]
    for copy in copies:
        copy.start()
    for copy in copies:
        copy.wait()


def per_device(mesh, *args):
    inputs, w_query, w_key, w_value, w_beta, beta_bias, cotangent = args
    nz = mesh.shape["head"]
    ny = nz
    nj = mesh.shape["seq"] // ny
    tok, fb = inputs.shape
    rw, width = w_query.shape
    vp = width // nj
    ne = nj // 2
    vmem = pl.BlockSpec(memory_space=pltpu.VMEM)
    hbm = pl.BlockSpec(memory_space=pl.ANY)
    dma = pltpu.SemaphoreType.DMA
    scratch = [
        pltpu.VMEM((tok, width), F32),
        pltpu.VMEM((rw, width), F32),
        pltpu.VMEM((rw, width), F32),
        pltpu.VMEM((rw, width), F32),
        pltpu.VMEM((1, rw), F32),
        pltpu.VMEM((tok, width), F32),
        pltpu.VMEM((1, rw), BF16),
        pltpu.VMEM((nj, ny, 3 * rw, width), BF16),
        pltpu.VMEM((ny, 16, 128), BF16),
        pltpu.VMEM((nj, 16, 128), BF16),
        pltpu.VMEM((nz, tok, fb), BF16),
        pltpu.VMEM((nj, nz * rw, tok), BF16),
        pltpu.VMEM((nj, nz * rw, tok), BF16),
        pltpu.VMEM((nj, width, width), F32),
        pltpu.VMEM((nj, 2, vp, width), F32),
        pltpu.VMEM((nj, 2, vp, width), F32),
        pltpu.VMEM((2, vp, width), F32),
        pltpu.VMEM((2, ny, width // 2, width), BF16),
        pltpu.VMEM((ny, vp, width), F32),
        pltpu.VMEM((nj, 2, vp, width), F32),
        pltpu.VMEM((nj, 2, vp, width), F32),
        pltpu.VMEM((3, tok, width), BF16),
        pltpu.VMEM((nj, 3, tok, width), BF16),
        pltpu.VMEM((16, tok), BF16),
        pltpu.VMEM((nj, 16, tok), BF16),
        pltpu.VMEM((3, ny, rw, width), BF16),
        pltpu.VMEM((3, ny, rw, width), BF16),
        pltpu.VMEM((fb // 128, 8, 128), F32),
        pltpu.VMEM((ny, 8, 128), F32),
        dma((11,)),
        dma((nz,)), dma((nz,)),
        dma((ny,)), dma((ny,)),
        dma((ne, ny)), dma((ne, ny)),
        dma((ne, ny)), dma((ne, ny)),
        dma((ny,)), dma((ny,)),
        dma((ne,)), dma((ne,)),
        dma((ne,)), dma((ne,)),
        dma((ne,)), dma((ne,)),
        dma((ne,)), dma((ne,)),
        dma((nj,)), dma((nj,)),
        dma((ny,)), dma((ny,)),
        dma((ny,)), dma((ny,)),
        dma((1,)), dma((1,)),
        dma((nj,)), dma((nj,)),
        dma((nj,)), dma((nj,)),
        dma((4, ne)), dma((4, ne)),
        dma((4, ne)), dma((4, ne)),
        dma((3, ny)), dma((3, ny)),
        dma((ny,)), dma((ny,)),
    ]
    results = pl.pallas_call(
        functools.partial(kernel, nz, ny, nj),
        out_shape=(
            jax.ShapeDtypeStruct((tok, width), F32),
            jax.ShapeDtypeStruct((rw, width), F32),
            jax.ShapeDtypeStruct((rw, width), F32),
            jax.ShapeDtypeStruct((rw, width), F32),
            jax.ShapeDtypeStruct((1, rw), F32),
        ),
        in_specs=[hbm, hbm, hbm, hbm, hbm, pl.BlockSpec(memory_space=pltpu.SMEM), hbm],
        out_specs=(hbm,) * 5,
        scratch_shapes=scratch,
        compiler_params=pltpu.CompilerParams(
            collective_id=0, has_side_effects=True, vmem_limit_bytes=60 * 1024 * 1024
        ),
        name="delta_step",
    )(inputs, w_query, w_key, w_value, w_beta.reshape(1, rw), beta_bias, cotangent)
    results = pl.pallas_call(
        write_out,
        out_shape=[jax.ShapeDtypeStruct(r.shape, F32) for r in results],
        in_specs=[vmem] * 5,
        out_specs=[hbm] * 5,
        scratch_shapes=[dma((5,))],
        name="write_out",
    )(*results)
    return (results[0], results[1], results[2], results[3], results[4].reshape(rw, 1))


def solution(mesh):
    return jax.shard_map(
        functools.partial(per_device, mesh),
        mesh=mesh,
        in_specs=(P("seq", "head"),) * 5 + (P("head"), P("seq", "head")),
        out_specs=(P("seq", "head"),) * 5,
        check_vma=False,
    )
```

```python
import functools
import math

import jax
import jax.numpy as jnp
from jax import lax
from jax.experimental import pallas as pl
from jax.experimental.pallas import tpu as pltpu
from jax.sharding import PartitionSpec as P

MESH = pl.DeviceIdType.MESH
F32 = jnp.float32
BF16 = jnp.bfloat16
NN = (((1,), (0,)), ((), ()))
NT = (((1,), (1,)), ((), ()))


def split(a):
    high = a.astype(BF16)
    return high, (a - high.astype(F32)).astype(BF16)


def mm(a, b, form=NN):
    a_high, a_low = split(a)
    b_high, b_low = split(b)
    return mm1(a_high, b_high, form) + (mm1(a_high, b_low, form) + mm1(a_low, b_high, form))


def mm1(a, b, form=NN):
    return lax.dot_general(a, b, form, preferred_element_type=F32)


def kernel(
    nz, ny, nj,
    x_ref, wq_ref, wk_ref, wv_ref, wb_ref, bias_ref, cot_ref,
    o_out, gq_out, gk_out, gv_out, gb_out,
    o_ref, gq_ref, gk_ref, gv_ref, gb_ref, cotv, wbv, wg, wq, wb1, wb2, xg, xt, xr, ag, bcs, bcr, gbc, ya, ybc, sgs, sgr, ggs, gg, gbs, gbr, ps, pr, pbs, pbr,
    ls, zs, zr, w1s, w1r, w2s, w2r, w3s, w3r, q1s, q1r, q2s, q2r, q3s, q3r, v1s, v1r, v2s, v2r, v3s, v3r, as_, ar, ass, asr, bs, br, y1s, y1r, y2s, y2r, y3s, y3r,
    xs, xrs, ss, sr, gs, grs, hs, hr, ps_, prs, pbs_, pbrs,
):
    h = lax.axis_index("head")
    s = lax.axis_index("seq")
    y = s // nj
    j = lax.rem(s, nj)
    core = lax.rem(j, 2)
    tok, fb = x_ref.shape
    rw, width = wq_ref.shape
    vp = width // nj

    def zdev(d):
        return (lax.rem(h + d + nz, nz), s)

    def yat(d):
        return lax.rem(y + d + ny, ny)

    def ydev(d):
        return (h, yat(d) * nj + j)

    def jat(d):
        return lax.rem(j + d + nj, nj)

    def jdev(d):
        return (h, y * nj + jat(d))

    sib = j + 1 - 2 * core
    sibdev = (h, y * nj + sib)
    sent = []

    def drain():
        for copy in sent:
            copy.wait_send()
        del sent[:]

    def push(src, dst, sems, at, dev):
        copy = pltpu.make_async_remote_copy(
            src_ref=src, dst_ref=dst, send_sem=sems[0].at[at], recv_sem=sems[1].at[at], device_id=dev, device_id_type=MESH
        )
        copy.start()
        sent.append(copy)

    def arrived(dst, sems, at):
        pltpu.make_async_remote_copy(
            src_ref=dst, dst_ref=dst, send_sem=sems[0].at[at], recv_sem=sems[1].at[at], device_id=sibdev, device_id_type=MESH
        ).wait_recv()

    local = [
        pltpu.make_async_copy(x_ref, xg.at[h], ls.at[0]),
        pltpu.make_async_copy(wq_ref, wq.at[j, y, pl.ds(0, rw)], ls.at[1]),
        pltpu.make_async_copy(wk_ref, wg.at[j, y], ls.at[2]),
        pltpu.make_async_copy(wv_ref, wq.at[j, y, pl.ds(rw, rw)], ls.at[3]),
        pltpu.make_async_copy(cot_ref, cotv, ls.at[4]),
        pltpu.make_async_copy(wb_ref, wbv, ls.at[10]),
    ]
    for copy in local:
        copy.start()

    barrier = pltpu.get_barrier_semaphore()
    for d in (-1, -2):
        pl.semaphore_signal(barrier, inc=1, device_id=zdev(d), device_id_type=MESH)
    for d in (1, 2):
        @pl.when(h + d < nz)
        def _():
            pl.semaphore_signal(barrier, inc=1, device_id=zdev(d), device_id_type=MESH)
    for d in range(1, ny):
        pl.semaphore_signal(barrier, inc=1, device_id=ydev(d), device_id_type=MESH)
    for d in range(1, nj):
        pl.semaphore_signal(barrier, inc=1, device_id=jdev(d), device_id_type=MESH)

    per = 128 // rw
    lane = lax.broadcasted_iota(jnp.int32, (1, 128), 1)
    for copy in local:
        copy.wait()
    wb_row = jnp.concatenate([wbv[...].astype(F32)] * per, axis=1)
    wb_row = jnp.where(lane // rw == lax.rem(j, per), wb_row, 0.0)
    wb1[y] = jnp.broadcast_to(wb_row, (16, 128)).astype(BF16)

    pl.semaphore_wait(barrier, ny + nj + 2 - jnp.maximum(2 - h, 0))

    order_y = sorted(range(1, ny), key=lambda d: min(d, ny - d))
    order_j = sorted(range(1, nj), key=lambda d: min(d, nj - d))
    evens = [e for e in order_j if e % 2 == 0]

    for d in order_y:
        push(wg.at[j, y], wg.at[j, y], (w1s, w1r), (d,), ydev(d))
    for n, e in enumerate(evens):
        push(wg.at[j, y], wg.at[j, y], (w2s, w2r), (n, 0), jdev(e))
    up, down = lax.rem(h - 2 + nz, nz), lax.rem(h + 2, nz)
    mid = tok // 2

    def send(src, at, d):
        copy = pltpu.make_async_remote_copy(
            src_ref=src, dst_ref=src, send_sem=zs.at[at], recv_sem=zr.at[at],
            device_id=zdev(d), device_id_type=MESH,
        )
        return copy

    def z_copies():
        return {
            2: send(xg.at[h], 2, 2),
            1: send(xg.at[h], 1, 1),
            -2: send(xg.at[h], nz - 2, -2),
            -1: send(xg.at[h], nz - 1, -1),
            3: send(xg.at[up], 3, 1),
            4: send(xg.at[up, pl.ds(0, mid)], 4, 2),
            -3: send(xg.at[down], nz - 3, -1),
            -4: send(xg.at[down, pl.ds(mid, mid)], 0, -2),
        }

    def got(d):
        return send(xg.at[lax.rem(h - d + nz, nz)], d % nz, 1).wait_recv

    z_copies()[2].start()
    z_copies()[1].start()

    @pl.when(h >= 2)
    def _():
        z_copies()[-2].start()

    @pl.when(h >= 1)
    def _():
        z_copies()[-1].start()

    def pass_up():
        got(2)()
        z_copies()[3].start()
        z_copies()[4].start()

    def pass_down():
        got(1)()
        got(-2)()
        z_copies()[-3].start()
        z_copies()[-4].start()
    for d in order_y:
        push(wb1.at[y], wb1.at[y], (v1s, v1r), (d,), ydev(d))
    for d in order_y:
        push(wq.at[j, y], wq.at[j, y], (q1s, q1r), (d,), ydev(d))
    push(wg.at[j, y], wg.at[j, y], (w3s, w3r), (0, 0), sibdev)

    def take_w(d):
        part = wg.at[j, yat(-d)]
        arrived(part, (w1s, w1r), (d,))
        for n, e in enumerate(evens):
            push(part, part, (w2s, w2r), (n, d), jdev(e))
        push(part, part, (w3s, w3r), (0, d), sibdev)

    for d in order_y[:4]:
        take_w(d)
    @pl.when(h >= 2)
    def _():
        pass_up()
        pass_down()

    for d in order_y[4:]:
        take_w(d)
    for d in order_y:
        arrived(wb1.at[yat(-d)], (v1s, v1r), (d,))
    turn = lax.broadcasted_iota(jnp.int32, (16, 128), 0)
    col = jnp.zeros((16, 128), F32)
    for b in range(ny):
        col = jnp.where(turn == b, wb1[b].astype(F32), col)
    wb2[j] = col.astype(BF16)
    push(wb2.at[j], wb2.at[j], (v3s, v3r), (0,), sibdev)
    for n, e in enumerate(evens):
        push(wb2.at[j], wb2.at[j], (v2s, v2r), (n,), jdev(e))

    for d in order_y:
        arrived(wq.at[j, yat(-d)], (q1s, q1r), (d,))
    for n, e in enumerate(evens):
        push(wq.at[j], wq.at[j], (q2s, q2r), (n,), jdev(e))
    push(wq.at[j], wq.at[j], (q3s, q3r), (0,), sibdev)

    @pl.when(h < 2)
    def _():
        pass_up()
        z_copies()[-2].start()

        @pl.when(h < 1)
        def _():
            got(1)()
            z_copies()[-1].start()

        @pl.when(h >= 1)
        def _():
            got(1)()
        got(-2)()
        z_copies()[-3].start()
        z_copies()[-4].start()

    cot = cotv[...]
    cot_t = cot.T

    for d in [0] + order_y:
        for n, e in enumerate(evens):
            part = wg.at[jat(-e), yat(-d)]
            arrived(part, (w2s, w2r), (n, d))
            push(part, part, (w3s, w3r), (n + 1, d), sibdev)
    for n, e in enumerate(evens):
        part = wb2.at[jat(-e)]
        arrived(part, (v2s, v2r), (n,))
        push(part, part, (v3s, v3r), (n + 1,), sibdev)
    for d in (-1, 3, -3):
        got(d)()
    far = lax.rem(h + 4, nz)
    send(xg.at[far, pl.ds(0, mid)], 4, 2).wait_recv()
    send(xg.at[far, pl.ds(mid, mid)], 0, -2).wait_recv()
    for n, e in enumerate([0] + evens):
        part = lax.rem(sib - e + nj, nj)
        for d in [0] + order_y:
            arrived(wg.at[part, yat(-d)], (w3s, w3r), (n, d))
        arrived(wb2.at[part], (v3s, v3r), (n,))

    raw = jnp.zeros((tok, width), F32)
    lacc = jnp.zeros((tok, 128), F32)
    w_rows = [
        jnp.sum(wb2[g * per:(g + 1) * per].astype(F32), axis=0) for g in range(fb // 128)
    ]
    for b in range(nz):
        xb = xg[b]
        raw = raw + mm1(xb, wg[:, b].reshape(fb, width))
        for g in range(fb // 128):
            lacc = lacc + xb[:, g * 128:(g + 1) * 128].astype(F32) * w_rows[g][b:b + 1]
    logit = jnp.sum(lacc, axis=1, keepdims=True) + bias_ref[0]
    beta = 2.0 * jax.nn.sigmoid(logit)

    def unit(r):
        scale = lax.rsqrt(jnp.mean(r * r, axis=1, keepdims=True) + 1e-06) * (1.0 / math.sqrt(width))
        return r * scale, scale

    k, k_scale = unit(raw)
    ri = lax.broadcasted_iota(jnp.int32, (tok, tok), 0)
    ci = lax.broadcasted_iota(jnp.int32, (tok, tok), 1)
    lower = ri > ci
    upper = ri < ci
    lower_d = ri >= ci
    upper_d = ri <= ci
    eye = jnp.where(ri == ci, 1.0, 0.0).astype(F32)

    gram = mm(k, k, NT)
    low = jnp.where(lower, beta * gram, 0.0)
    first = jnp.where((ri // 4) == (ci // 4), low, 0.0)
    t_mat = eye - first
    t_mat = t_mat + mm(t_mat, mm(first, first))
    size = 4
    while size < tok:
        if 2 * size == tok:
            for n, e in enumerate(evens):
                part = wq.at[jat(-e)]
                arrived(part, (q2s, q2r), (n,))
                push(part, part, (q3s, q3r), (n + 1,), sibdev)
        wide = min(4 * size, tok)
        level = ((ri // wide) == (ci // wide)) & ((ri // size) != (ci // size))
        step = mm(jnp.where(level, low, 0.0), t_mat)
        if wide == 4 * size:
            square = mm(step, step)
            t_mat = t_mat - mm(t_mat, step)
            t_mat = t_mat + mm(t_mat, square)
        else:
            t_mat = t_mat - mm(t_mat, step)
        size = wide
    k_t = k.T
    w_mat = mm(t_mat, beta * k)
    ag[j] = eye - mm(k_t, w_mat)
    push(ag.at[j], ag.at[j], (ass, asr), (0,), sibdev)
    for n, e in enumerate(evens):
        push(ag.at[j], ag.at[j], (as_, ar), (n,), jdev(e))

    for n, e in enumerate([0] + evens):
        arrived(wq.at[lax.rem(sib - e + nj, nj)], (q3s, q3r), (n,))
    raw = jnp.zeros((tok, 2 * width), F32)
    for b in range(nz):
        w_b = jnp.concatenate(
            [wq[:, b, m * rw:(m + 1) * rw, :].reshape(fb, width) for m in range(2)], axis=1
        )
        raw = raw + mm1(xg[b], w_b)
    q, q_scale = unit(raw[:, :width])
    v = raw[:, width:]
    m_mat = jnp.where(lower_d, mm(q, k, NT), 0.0)
    q_eff = q - mm(m_mat, w_mat)
    u_mat = mm(t_mat, beta * v)
    bcs[:, 0] = mm(k_t, u_mat).T.reshape(nj, vp, width)
    bcs[:, 1] = mm(cot_t, q_eff).reshape(nj, vp, width)
    bcr[j] = bcs[j]
    for d in order_j:
        push(bcs.at[jat(d)], bcr.at[j], (bs, br), (d,), jdev(d))

    m_t = jnp.where(upper_d, mm(k, q, NT), 0.0)
    ty = mm(t_mat.T, jnp.concatenate([k, mm(m_t, cot)], axis=1))
    t_k, y_0 = ty[:, :width], ty[:, width:]
    m_u = mm(m_mat, u_mat)
    for b in range(nz):
        xt[:, b * rw:(b + 1) * rw, :] = xg[b].astype(F32).T.astype(BF16).reshape(nj, rw, tok)

    drain()
    for copy in z_copies().values():
        copy.wait_send()
    for n, e in enumerate(evens):
        part = ag.at[jat(-e)]
        arrived(part, (as_, ar), (n,))
        push(part, part, (ass, asr), (n + 1,), sibdev)
    arrived(ag.at[sib], (ass, asr), (0,))
    for n, e in enumerate(evens):
        arrived(ag.at[lax.rem(sib - e + nj, nj)], (ass, asr), (n + 1,))
    for d in order_j:
        arrived(bcr.at[jat(-d)], (bs, br), (d,))

    pair_p, pair_b, pair_c = [], [], []
    for i in range(0, nj, 2):
        pair_p.append(mm(ag[i + 1], ag[i]))
        pair_b.append(mm(bcr[i, 0], ag[i + 1], NT) + bcr[i + 1, 0])
        pair_c.append(mm(bcr[i + 1, 1], ag[i]) + bcr[i, 1])
    p_mat, b_row, c_row = pair_p[0], pair_b[0], pair_c[-1]
    befores = [None, ag[0], p_mat]
    b_before = [None, bcr[0, 0], b_row]
    c_after = {nj - 2: bcr[nj - 1, 1], nj - 3: c_row}
    for i in range(1, nj // 2):
        back = nj // 2 - 1 - i
        p_mat = mm(pair_p[i], p_mat)
        b_row = mm(b_row, pair_p[i], NT) + pair_b[i]
        c_row = mm(c_row, pair_p[back]) + pair_c[back]
        befores += [None, p_mat]
        b_before += [None, b_row]
        c_after[2 * back - 1] = c_row
    ybc[y] = jnp.zeros((vp, width), F32)
    gbc[0] = b_row
    gbc[1] = c_row
    half = tok // 2
    top, bottom = p_mat[:half].astype(BF16), p_mat[half:].astype(BF16)
    ya[core, y] = jnp.where(core == 0, top, bottom)
    for d in order_y:
        push(ya.at[core, y], ya.at[core, y], (y1s, y1r), (d,), ydev(d))
        side = (y + d) // ny
        push(gbc.at[side], ybc.at[y], (y2s, y2r), (d,), ydev(d))
    for d in order_j:
        xr_dst = xr.at[j]
        push(xt.at[jat(d)], xr_dst, (xs, xrs), (d,), jdev(d))
    xr[j] = xt[j]

    afters = {nj - 2: ag[nj - 1], nj - 3: pair_p[-1]}
    for i in range(nj // 2 - 2, -1, -1):
        afters[2 * i - 1] = mm(afters[2 * i + 1], pair_p[i])
        afters[2 * i] = mm(afters[2 * i + 1], ag[2 * i + 1])
        c_after[2 * i] = mm(c_after[2 * i + 1], ag[2 * i + 1]) + bcr[2 * i + 1, 1]
        m = nj - 2 - 2 * i
        befores[m + 1] = mm(ag[m], befores[m])
        b_before[m + 1] = mm(b_before[m], ag[m], NT) + bcr[m, 0]
    drain()
    for d in order_y:
        arrived(ya.at[core, yat(-d)], (y1s, y1r), (d,))
    push(ya.at[core], ya.at[core], (y3s, y3r), (0,), sibdev)
    for d in order_y:
        arrived(ybc.at[yat(-d)], (y2s, y2r), (d,))
    arrived(ya.at[1 - core], (y3s, y3r), (0,))

    def full(t):
        return jnp.concatenate([ya[0, t], ya[1, t]], axis=0).astype(F32)

    s_g = jnp.zeros((vp, width), F32)
    g_g = jnp.zeros((vp, width), F32)
    for t in range(ny - 1):
        s_g = jnp.where(t < y, mm(s_g, full(t), NT) + ybc[t], s_g)
        u = ny - 1 - t
        g_g = jnp.where(u > y, mm(g_g, full(u)) + ybc[u], g_g)

    sgs[0, 0] = s_g
    sgs[nj - 1, 1] = g_g
    for i in range(1, nj):
        sgs[i, 0] = mm(s_g, befores[i], NT) + b_before[i]
    for i in range(nj - 1):
        sgs[i, 1] = mm(g_g, afters[i]) + c_after[i]
    for d in order_j:
        push(sgs.at[jat(d)], sgr.at[j], (ss, sr), (d,), jdev(d))
    sgr[j] = sgs[j]
    drain()
    for d in order_j:
        arrived(sgr.at[jat(-d)], (ss, sr), (d,))

    state = sgr[:, 0].reshape(width, width)
    grad = sgr[:, 1].reshape(width, width)
    y_mat = y_0 + mm(t_k, grad, NT)
    b_y = beta * y_mat
    ggs[2] = b_y.astype(BF16)

    def share(src, dst, m):
        push(src, dst, (hs, hr), (m, 0), sibdev)
        for n, e in enumerate(evens):
            push(src, dst, (gs, grs), (m, n), jdev(e))

    def shared(at, m):
        for n, e in enumerate(evens):
            part = at(jat(-e))
            arrived(part, (gs, grs), (m, n))
            push(part, part, (hs, hr), (m, n + 1), sibdev)

    def collected(at, m):
        for n, e in enumerate([0] + evens):
            arrived(at(lax.rem(sib - e + nj, nj)), (hs, hr), (m, n))

    gg[j, 2] = ggs[2]
    share(ggs.at[2], gg.at[j, 2], 2)
    fresh = u_mat - mm(w_mat, state, NT)
    o_ref[...] = mm(q_eff, state, NT) + m_u
    stores = [pltpu.make_async_copy(o_ref, o_out, ls.at[5])]
    stores[0].start()
    d_m = jnp.where(lower_d, mm(cot, fresh, NT), 0.0)
    d_q = mm(cot, state) + mm(d_m, k)
    ggs[0] = (q_scale * (d_q - q * jnp.sum(d_q * q, axis=1, keepdims=True))).astype(BF16)
    gg[j, 0] = ggs[0]
    share(ggs.at[0], gg.at[j, 0], 0)
    rest = v - mm(k, state, NT)
    d_mt = jnp.where(upper_d, mm(fresh, cot, NT), 0.0)
    yd = jnp.where(lower, mm(y_mat, fresh, NT), 0.0)
    both = beta * yd + jnp.where(upper, mm(fresh, b_y, NT), 0.0)
    d_k = mm(fresh, grad) - mm(b_y, state) + mm(d_mt, q) - mm(both, k)
    ggs[1] = (k_scale * (d_k - k * jnp.sum(d_k * k, axis=1, keepdims=True))).astype(BF16)
    gg[j, 1] = ggs[1]
    share(ggs.at[1], gg.at[j, 1], 1)
    d_beta = jnp.sum(y_mat * rest - yd * gram, axis=1, keepdims=True)
    d_logit = d_beta * beta * (1.0 - 0.5 * beta)
    dl_row = jnp.sum(eye * d_logit, axis=0, keepdims=True)
    gbs[...] = jnp.broadcast_to(dl_row, (16, tok)).astype(BF16)
    gbr[j] = gbs[...]
    share(gbs, gbr.at[j], 3)

    for d in order_j:
        arrived(xr.at[jat(-d)], (xs, xrs), (d,))
    x_t = jnp.concatenate([xr[i] for i in range(nj)], axis=1)

    outs = {0: gq_ref, 1: gk_ref, 2: gv_ref}
    places = [
        lambda i: gg.at[i, 0],
        lambda i: gg.at[i, 1],
        lambda i: gg.at[i, 2],
        lambda i: gbr.at[i],
    ]
    def spread(m):
        collected(places[m], m)
        part = mm1(x_t, gg[:, m].reshape(nj * tok, width)).reshape(ny, rw, width)
        pr[m, y] = jnp.zeros((rw, width), BF16)
        ps[m] = part.astype(BF16)
        for d in order_y:
            push(ps.at[m, yat(d)], pr.at[m, y], (ps_, prs), (m, d), ydev(d))
        own = part[0]
        for t in range(1, ny):
            own = jnp.where(t == y, part[t], own)
        outs[m][...] = own

    for m in (2, 0, 1, 3):
        shared(places[m], m)
    for m in (2, 0, 1):
        spread(m)
    collected(places[3], 3)
    pb = mm1(jnp.concatenate([gbr[i] for i in range(nj)], axis=1), x_t, NT)
    for g in range(fb // 128):
        pbs[g] = pb[:8, g * 128:(g + 1) * 128]
    for d in order_y:
        push(pbs.at[yat(d) * rw // 128], pbr.at[y], (pbs_, pbrs), (d,), ydev(d))
    pbr[y] = pbs[y * rw // 128]

    def store(src, dst, at):
        stores.append(pltpu.make_async_copy(src, dst, ls.at[at]))
        stores[-1].start()

    out_refs = {0: gq_out, 1: gk_out, 2: gv_out}
    for m in (2, 0, 1):
        for d in order_y:
            arrived(pr.at[m, yat(-d)], (ps_, prs), (m, d))
        outs[m][...] += jnp.sum(pr[m].astype(F32), axis=0)
        store(outs[m], out_refs[m], 6 + m)
    for d in order_y:
        arrived(pbr.at[yat(-d)], (pbs_, pbrs), (d,))
    pb_row = jnp.sum(pbr[...], axis=0)[:1]
    gb_row = jnp.zeros((1, rw), F32)
    for g in range(per):
        gb_row = jnp.where(lax.rem(y, per) == g, pb_row[:, g * rw:(g + 1) * rw], gb_row)
    gb_ref[...] = gb_row
    store(gb_ref, gb_out, 9)

    drain()
    for copy in stores:
        copy.wait()


def write_out(o_in, gq_in, gk_in, gv_in, gb_in, o_out, gq_out, gk_out, gv_out, gb_out, sems):
    pairs = [(o_in, o_out), (gq_in, gq_out), (gk_in, gk_out), (gv_in, gv_out), (gb_in, gb_out)]
    copies = [pltpu.make_async_copy(pairs[i][0], pairs[i][1], sems.at[i]) for i in range(5)]
    for copy in copies:
        copy.start()
    for copy in copies:
        copy.wait()


def per_device(mesh, *args):
    inputs, w_query, w_key, w_value, w_beta, beta_bias, cotangent = args
    nz = mesh.shape["head"]
    ny = nz
    nj = mesh.shape["seq"] // ny
    tok, fb = inputs.shape
    rw, width = w_query.shape
    vp = width // nj
    ne = nj // 2
    vmem = pl.BlockSpec(memory_space=pltpu.VMEM)
    hbm = pl.BlockSpec(memory_space=pl.ANY)
    dma = pltpu.SemaphoreType.DMA
    scratch = [
        pltpu.VMEM((tok, width), F32),
        pltpu.VMEM((rw, width), F32),
        pltpu.VMEM((rw, width), F32),
        pltpu.VMEM((rw, width), F32),
        pltpu.VMEM((1, rw), F32),
        pltpu.VMEM((tok, width), F32),
        pltpu.VMEM((1, rw), BF16),
        pltpu.VMEM((nj, ny, rw, width), BF16),
        pltpu.VMEM((nj, ny, 2 * rw, width), BF16),
        pltpu.VMEM((ny, 16, 128), BF16),
        pltpu.VMEM((nj, 16, 128), BF16),
        pltpu.VMEM((nz, tok, fb), BF16),
        pltpu.VMEM((nj, nz * rw, tok), BF16),
        pltpu.VMEM((nj, nz * rw, tok), BF16),
        pltpu.VMEM((nj, width, width), F32),
        pltpu.VMEM((nj, 2, vp, width), F32),
        pltpu.VMEM((nj, 2, vp, width), F32),
        pltpu.VMEM((2, vp, width), F32),
        pltpu.VMEM((2, ny, width // 2, width), BF16),
        pltpu.VMEM((ny, vp, width), F32),
        pltpu.VMEM((nj, 2, vp, width), F32),
        pltpu.VMEM((nj, 2, vp, width), F32),
        pltpu.VMEM((3, tok, width), BF16),
        pltpu.VMEM((nj, 3, tok, width), BF16),
        pltpu.VMEM((16, tok), BF16),
        pltpu.VMEM((nj, 16, tok), BF16),
        pltpu.VMEM((3, ny, rw, width), BF16),
        pltpu.VMEM((3, ny, rw, width), BF16),
        pltpu.VMEM((fb // 128, 8, 128), F32),
        pltpu.VMEM((ny, 8, 128), F32),
        dma((11,)),
        dma((nz,)), dma((nz,)),
        dma((ny,)), dma((ny,)),
        dma((ne, ny)), dma((ne, ny)),
        dma((ne, ny)), dma((ne, ny)),
        dma((ny,)), dma((ny,)),
        dma((ne,)), dma((ne,)),
        dma((ne,)), dma((ne,)),
        dma((ny,)), dma((ny,)),
        dma((ne,)), dma((ne,)),
        dma((ne,)), dma((ne,)),
        dma((ne,)), dma((ne,)),
        dma((ne,)), dma((ne,)),
        dma((nj,)), dma((nj,)),
        dma((ny,)), dma((ny,)),
        dma((ny,)), dma((ny,)),
        dma((1,)), dma((1,)),
        dma((nj,)), dma((nj,)),
        dma((nj,)), dma((nj,)),
        dma((4, ne)), dma((4, ne)),
        dma((4, ne)), dma((4, ne)),
        dma((3, ny)), dma((3, ny)),
        dma((ny,)), dma((ny,)),
    ]
    results = pl.pallas_call(
        functools.partial(kernel, nz, ny, nj),
        out_shape=(
            jax.ShapeDtypeStruct((tok, width), F32),
            jax.ShapeDtypeStruct((rw, width), F32),
            jax.ShapeDtypeStruct((rw, width), F32),
            jax.ShapeDtypeStruct((rw, width), F32),
            jax.ShapeDtypeStruct((1, rw), F32),
        ),
        in_specs=[hbm, hbm, hbm, hbm, hbm, pl.BlockSpec(memory_space=pltpu.SMEM), hbm],
        out_specs=(hbm,) * 5,
        scratch_shapes=scratch,
        compiler_params=pltpu.CompilerParams(
            collective_id=0, has_side_effects=True, vmem_limit_bytes=60 * 1024 * 1024
        ),
        name="delta_step",
    )(inputs, w_query, w_key, w_value, w_beta.reshape(1, rw), beta_bias, cotangent)
    results = pl.pallas_call(
        write_out,
        out_shape=[jax.ShapeDtypeStruct(r.shape, F32) for r in results],
        in_specs=[vmem] * 5,
        out_specs=[hbm] * 5,
        scratch_shapes=[dma((5,))],
        name="write_out",
    )(*results)
    return (results[0], results[1], results[2], results[3], results[4].reshape(rw, 1))


def solution(mesh):
    return jax.shard_map(
        functools.partial(per_device, mesh),
        mesh=mesh,
        in_specs=(P("seq", "head"),) * 5 + (P("head"), P("seq", "head")),
        out_specs=(P("seq", "head"),) * 5,
        check_vma=False,
    )
```

```python
import functools
import math

import jax
import jax.numpy as jnp
from jax import lax
from jax.experimental import pallas as pl
from jax.experimental.pallas import tpu as pltpu
from jax.sharding import PartitionSpec as P

MESH = pl.DeviceIdType.MESH
F32 = jnp.float32
BF16 = jnp.bfloat16
NN = (((1,), (0,)), ((), ()))
NT = (((1,), (1,)), ((), ()))


def split(a):
    high = a.astype(BF16)
    return high, (a - high.astype(F32)).astype(BF16)


def mm(a, b, form=NN):
    a_high, a_low = split(a)
    b_high, b_low = split(b)
    return mm1(a_high, b_high, form) + (mm1(a_high, b_low, form) + mm1(a_low, b_high, form))


def mm1(a, b, form=NN):
    return lax.dot_general(a, b, form, preferred_element_type=F32)


def kernel(
    nz, ny, nj,
    x_ref, wq_ref, wk_ref, wv_ref, wb_ref, bias_ref, cot_ref,
    o_out, gq_out, gk_out, gv_out, gb_out,
    o_ref, gq_ref, gk_ref, gv_ref, gb_ref, cotv, wbv, wg, wq, wb1, wb2, xg, xt, xr, ag, bcs, bcr, gbc, ya, ybc, sgs, sgr, ggs, gg, gbs, gbr, ps, pr, pbs, pbr,
    ls, zs, zr, w1s, w1r, w2s, w2r, w3s, w3r, q1s, q1r, q2s, q2r, q3s, q3r, v1s, v1r, v2s, v2r, v3s, v3r, as_, ar, ass, asr, bs, br, y1s, y1r, y2s, y2r, y3s, y3r,
    xs, xrs, ss, sr, gs, grs, hs, hr, ps_, prs, pbs_, pbrs,
):
    h = lax.axis_index("head")
    s = lax.axis_index("seq")
    y = s // nj
    j = lax.rem(s, nj)
    core = lax.rem(j, 2)
    tok, fb = x_ref.shape
    rw, width = wq_ref.shape
    vp = width // nj

    def zdev(d):
        return (lax.rem(h + d + nz, nz), s)

    def yat(d):
        return lax.rem(y + d + ny, ny)

    def ydev(d):
        return (h, yat(d) * nj + j)

    def jat(d):
        return lax.rem(j + d + nj, nj)

    def jdev(d):
        return (h, y * nj + jat(d))

    sib = j + 1 - 2 * core
    sibdev = (h, y * nj + sib)
    sent = []

    def drain():
        for copy in sent:
            copy.wait_send()
        del sent[:]

    def push(src, dst, sems, at, dev):
        copy = pltpu.make_async_remote_copy(
            src_ref=src, dst_ref=dst, send_sem=sems[0].at[at], recv_sem=sems[1].at[at], device_id=dev, device_id_type=MESH
        )
        copy.start()
        sent.append(copy)

    def arrived(dst, sems, at):
        pltpu.make_async_remote_copy(
            src_ref=dst, dst_ref=dst, send_sem=sems[0].at[at], recv_sem=sems[1].at[at], device_id=sibdev, device_id_type=MESH
        ).wait_recv()

    local = [
        pltpu.make_async_copy(x_ref, xg.at[h], ls.at[0]),
        pltpu.make_async_copy(wq_ref, wq.at[j, y, pl.ds(0, rw)], ls.at[1]),
        pltpu.make_async_copy(wk_ref, wg.at[j, y], ls.at[2]),
        pltpu.make_async_copy(wv_ref, wq.at[j, y, pl.ds(rw, rw)], ls.at[3]),
        pltpu.make_async_copy(cot_ref, cotv, ls.at[4]),
        pltpu.make_async_copy(wb_ref, wbv, ls.at[10]),
    ]
    for copy in local:
        copy.start()

    barrier = pltpu.get_barrier_semaphore()
    for d in (-1, -2):
        pl.semaphore_signal(barrier, inc=1, device_id=zdev(d), device_id_type=MESH)
    for d in (1, 2):
        @pl.when(h + d < nz)
        def _():
            pl.semaphore_signal(barrier, inc=1, device_id=zdev(d), device_id_type=MESH)
    for d in range(1, ny):
        pl.semaphore_signal(barrier, inc=1, device_id=ydev(d), device_id_type=MESH)
    for d in range(1, nj):
        pl.semaphore_signal(barrier, inc=1, device_id=jdev(d), device_id_type=MESH)

    per = 128 // rw
    lane = lax.broadcasted_iota(jnp.int32, (1, 128), 1)
    for copy in local:
        copy.wait()
    wb_row = jnp.concatenate([wbv[...].astype(F32)] * per, axis=1)
    wb_row = jnp.where(lane // rw == lax.rem(j, per), wb_row, 0.0)
    wb1[y] = jnp.broadcast_to(wb_row, (16, 128)).astype(BF16)

    pl.semaphore_wait(barrier, ny + nj + 2 - jnp.maximum(2 - h, 0))

    order_y = sorted(range(1, ny), key=lambda d: min(d, ny - d))
    order_j = sorted(range(1, nj), key=lambda d: min(d, nj - d))
    evens = [e for e in order_j if e % 2 == 0]
    far_y, far_j = order_y[::-1], order_j[::-1]
    far_evens = [(n, e) for n, e in enumerate(evens)][::-1]

    for d in order_y:
        push(wg.at[j, y], wg.at[j, y], (w1s, w1r), (d,), ydev(d))
    for n, e in enumerate(evens):
        push(wg.at[j, y], wg.at[j, y], (w2s, w2r), (n, 0), jdev(e))
    up, down = lax.rem(h - 2 + nz, nz), lax.rem(h + 2, nz)
    mid = tok // 2

    def send(src, at, d):
        copy = pltpu.make_async_remote_copy(
            src_ref=src, dst_ref=src, send_sem=zs.at[at], recv_sem=zr.at[at],
            device_id=zdev(d), device_id_type=MESH,
        )
        return copy

    def z_copies():
        return {
            2: send(xg.at[h], 2, 2),
            1: send(xg.at[h], 1, 1),
            -2: send(xg.at[h], nz - 2, -2),
            -1: send(xg.at[h], nz - 1, -1),
            3: send(xg.at[up], 3, 1),
            4: send(xg.at[up, pl.ds(0, mid)], 4, 2),
            -3: send(xg.at[down], nz - 3, -1),
            -4: send(xg.at[down, pl.ds(mid, mid)], 0, -2),
        }

    def got(d):
        return send(xg.at[lax.rem(h - d + nz, nz)], d % nz, 1).wait_recv

    z_copies()[2].start()
    z_copies()[1].start()

    @pl.when(h >= 2)
    def _():
        z_copies()[-2].start()

    @pl.when(h >= 1)
    def _():
        z_copies()[-1].start()

    def pass_up():
        got(2)()
        z_copies()[3].start()
        z_copies()[4].start()

    def pass_down():
        got(1)()
        got(-2)()
        z_copies()[-3].start()
        z_copies()[-4].start()
    for d in order_y:
        push(wb1.at[y], wb1.at[y], (v1s, v1r), (d,), ydev(d))
    for d in order_y:
        push(wq.at[j, y], wq.at[j, y], (q1s, q1r), (d,), ydev(d))
    push(wg.at[j, y], wg.at[j, y], (w3s, w3r), (0, 0), sibdev)

    def take_w(d):
        part = wg.at[j, yat(-d)]
        arrived(part, (w1s, w1r), (d,))
        for n, e in enumerate(evens):
            push(part, part, (w2s, w2r), (n, d), jdev(e))
        push(part, part, (w3s, w3r), (0, d), sibdev)

    for d in order_y[:4]:
        take_w(d)
    @pl.when(h >= 2)
    def _():
        pass_up()
        pass_down()

    for d in order_y[4:]:
        take_w(d)
    for d in order_y:
        arrived(wb1.at[yat(-d)], (v1s, v1r), (d,))
    turn = lax.broadcasted_iota(jnp.int32, (16, 128), 0)
    col = jnp.zeros((16, 128), F32)
    for b in range(ny):
        col = jnp.where(turn == b, wb1[b].astype(F32), col)
    wb2[j] = col.astype(BF16)
    push(wb2.at[j], wb2.at[j], (v3s, v3r), (0,), sibdev)
    for n, e in enumerate(evens):
        push(wb2.at[j], wb2.at[j], (v2s, v2r), (n,), jdev(e))

    for d in order_y:
        arrived(wq.at[j, yat(-d)], (q1s, q1r), (d,))
    for n, e in enumerate(evens):
        push(wq.at[j], wq.at[j], (q2s, q2r), (n,), jdev(e))
    push(wq.at[j], wq.at[j], (q3s, q3r), (0,), sibdev)

    @pl.when(h < 2)
    def _():
        pass_up()
        z_copies()[-2].start()

        @pl.when(h < 1)
        def _():
            got(1)()
            z_copies()[-1].start()

        @pl.when(h >= 1)
        def _():
            got(1)()
        got(-2)()
        z_copies()[-3].start()
        z_copies()[-4].start()

    cot = cotv[...]
    cot_t = cot.T

    for d in [0] + order_y:
        for n, e in enumerate(evens):
            part = wg.at[jat(-e), yat(-d)]
            arrived(part, (w2s, w2r), (n, d))
            push(part, part, (w3s, w3r), (n + 1, d), sibdev)
    for n, e in enumerate(evens):
        part = wb2.at[jat(-e)]
        arrived(part, (v2s, v2r), (n,))
        push(part, part, (v3s, v3r), (n + 1,), sibdev)
    for d in (-1, 3, -3):
        got(d)()
    far = lax.rem(h + 4, nz)
    send(xg.at[far, pl.ds(0, mid)], 4, 2).wait_recv()
    send(xg.at[far, pl.ds(mid, mid)], 0, -2).wait_recv()
    for n, e in enumerate([0] + evens):
        part = lax.rem(sib - e + nj, nj)
        for d in [0] + order_y:
            arrived(wg.at[part, yat(-d)], (w3s, w3r), (n, d))
        arrived(wb2.at[part], (v3s, v3r), (n,))

    raw = jnp.zeros((tok, width), F32)
    lacc = jnp.zeros((tok, 128), F32)
    w_rows = [
        jnp.sum(wb2[g * per:(g + 1) * per].astype(F32), axis=0) for g in range(fb // 128)
    ]
    for b in range(nz):
        xb = xg[b]
        raw = raw + mm1(xb, wg[:, b].reshape(fb, width))
        for g in range(fb // 128):
            lacc = lacc + xb[:, g * 128:(g + 1) * 128].astype(F32) * w_rows[g][b:b + 1]
    logit = jnp.sum(lacc, axis=1, keepdims=True) + bias_ref[0]
    beta = 2.0 * jax.nn.sigmoid(logit)

    def unit(r):
        scale = lax.rsqrt(jnp.mean(r * r, axis=1, keepdims=True) + 1e-06) * (1.0 / math.sqrt(width))
        return r * scale, scale

    k, k_scale = unit(raw)
    ri = lax.broadcasted_iota(jnp.int32, (tok, tok), 0)
    ci = lax.broadcasted_iota(jnp.int32, (tok, tok), 1)
    lower = ri > ci
    upper = ri < ci
    lower_d = ri >= ci
    upper_d = ri <= ci
    eye = jnp.where(ri == ci, 1.0, 0.0).astype(F32)

    gram = mm(k, k, NT)
    low = jnp.where(lower, beta * gram, 0.0)
    first = jnp.where((ri // 4) == (ci // 4), low, 0.0)
    t_mat = eye - first
    t_mat = t_mat + mm(t_mat, mm(first, first))
    size = 4
    while size < tok:
        if 2 * size == tok:
            for n, e in enumerate(evens):
                part = wq.at[jat(-e)]
                arrived(part, (q2s, q2r), (n,))
                push(part, part, (q3s, q3r), (n + 1,), sibdev)
        wide = min(4 * size, tok)
        level = ((ri // wide) == (ci // wide)) & ((ri // size) != (ci // size))
        step = mm(jnp.where(level, low, 0.0), t_mat)
        if wide == 4 * size:
            square = mm(step, step)
            t_mat = t_mat - mm(t_mat, step)
            t_mat = t_mat + mm(t_mat, square)
        else:
            t_mat = t_mat - mm(t_mat, step)
        size = wide
    k_t = k.T
    w_mat = mm(t_mat, beta * k)
    ag[j] = eye - mm(k_t, w_mat)
    push(ag.at[j], ag.at[j], (ass, asr), (0,), sibdev)
    for n, e in far_evens:
        push(ag.at[j], ag.at[j], (as_, ar), (n,), jdev(e))

    for n, e in enumerate([0] + evens):
        arrived(wq.at[lax.rem(sib - e + nj, nj)], (q3s, q3r), (n,))
    raw = jnp.zeros((tok, 2 * width), F32)
    for b in range(nz):
        w_b = jnp.concatenate(
            [wq[:, b, m * rw:(m + 1) * rw, :].reshape(fb, width) for m in range(2)], axis=1
        )
        raw = raw + mm1(xg[b], w_b)
    q, q_scale = unit(raw[:, :width])
    v = raw[:, width:]
    m_mat = jnp.where(lower_d, mm(q, k, NT), 0.0)
    q_eff = q - mm(m_mat, w_mat)
    u_mat = mm(t_mat, beta * v)
    bcs[:, 0] = mm(k_t, u_mat).T.reshape(nj, vp, width)
    bcs[:, 1] = mm(cot_t, q_eff).reshape(nj, vp, width)
    bcr[j] = bcs[j]
    for d in far_j:
        push(bcs.at[jat(d)], bcr.at[j], (bs, br), (d,), jdev(d))

    m_t = jnp.where(upper_d, mm(k, q, NT), 0.0)
    ty = mm(t_mat.T, jnp.concatenate([k, mm(m_t, cot)], axis=1))
    t_k, y_0 = ty[:, :width], ty[:, width:]
    m_u = mm(m_mat, u_mat)
    for b in range(nz):
        xt[:, b * rw:(b + 1) * rw, :] = xg[b].astype(F32).T.astype(BF16).reshape(nj, rw, tok)

    drain()
    for copy in z_copies().values():
        copy.wait_send()
    for n, e in enumerate(evens):
        part = ag.at[jat(-e)]
        arrived(part, (as_, ar), (n,))
        push(part, part, (ass, asr), (n + 1,), sibdev)
    arrived(ag.at[sib], (ass, asr), (0,))
    for n, e in enumerate(evens):
        arrived(ag.at[lax.rem(sib - e + nj, nj)], (ass, asr), (n + 1,))
    for d in order_j:
        arrived(bcr.at[jat(-d)], (bs, br), (d,))

    pair_p, pair_b, pair_c = [], [], []
    for i in range(0, nj, 2):
        pair_p.append(mm(ag[i + 1], ag[i]))
        pair_b.append(mm(bcr[i, 0], ag[i + 1], NT) + bcr[i + 1, 0])
        pair_c.append(mm(bcr[i + 1, 1], ag[i]) + bcr[i, 1])
    p_mat, b_row, c_row = pair_p[0], pair_b[0], pair_c[-1]
    befores = [None, ag[0], p_mat]
    b_before = [None, bcr[0, 0], b_row]
    c_after = {nj - 2: bcr[nj - 1, 1], nj - 3: c_row}
    for i in range(1, nj // 2):
        back = nj // 2 - 1 - i
        p_mat = mm(pair_p[i], p_mat)
        b_row = mm(b_row, pair_p[i], NT) + pair_b[i]
        c_row = mm(c_row, pair_p[back]) + pair_c[back]
        befores += [None, p_mat]
        b_before += [None, b_row]
        c_after[2 * back - 1] = c_row
    ybc[y] = jnp.zeros((vp, width), F32)
    gbc[0] = b_row
    gbc[1] = c_row
    half = tok // 2
    top, bottom = p_mat[:half].astype(BF16), p_mat[half:].astype(BF16)
    ya[core, y] = jnp.where(core == 0, top, bottom)
    for d in far_y:
        push(ya.at[core, y], ya.at[core, y], (y1s, y1r), (d,), ydev(d))
        side = (y + d) // ny
        push(gbc.at[side], ybc.at[y], (y2s, y2r), (d,), ydev(d))
    for d in order_j:
        xr_dst = xr.at[j]
        push(xt.at[jat(d)], xr_dst, (xs, xrs), (d,), jdev(d))
    xr[j] = xt[j]

    afters = {nj - 2: ag[nj - 1], nj - 3: pair_p[-1]}
    for i in range(nj // 2 - 2, -1, -1):
        afters[2 * i - 1] = mm(afters[2 * i + 1], pair_p[i])
        afters[2 * i] = mm(afters[2 * i + 1], ag[2 * i + 1])
        c_after[2 * i] = mm(c_after[2 * i + 1], ag[2 * i + 1]) + bcr[2 * i + 1, 1]
        m = nj - 2 - 2 * i
        befores[m + 1] = mm(ag[m], befores[m])
        b_before[m + 1] = mm(b_before[m], ag[m], NT) + bcr[m, 0]
    drain()
    for d in order_y:
        arrived(ya.at[core, yat(-d)], (y1s, y1r), (d,))
    push(ya.at[core], ya.at[core], (y3s, y3r), (0,), sibdev)
    for d in order_y:
        arrived(ybc.at[yat(-d)], (y2s, y2r), (d,))
    arrived(ya.at[1 - core], (y3s, y3r), (0,))

    def full(t):
        return jnp.concatenate([ya[0, t], ya[1, t]], axis=0).astype(F32)

    s_g = jnp.zeros((vp, width), F32)
    g_g = jnp.zeros((vp, width), F32)
    for t in range(ny - 1):
        s_g = jnp.where(t < y, mm(s_g, full(t), NT) + ybc[t], s_g)
        u = ny - 1 - t
        g_g = jnp.where(u > y, mm(g_g, full(u)) + ybc[u], g_g)

    sgs[0, 0] = s_g
    sgs[nj - 1, 1] = g_g
    for i in range(1, nj):
        sgs[i, 0] = mm(s_g, befores[i], NT) + b_before[i]
    for i in range(nj - 1):
        sgs[i, 1] = mm(g_g, afters[i]) + c_after[i]
    for d in far_j:
        push(sgs.at[jat(d)], sgr.at[j], (ss, sr), (d,), jdev(d))
    sgr[j] = sgs[j]
    drain()
    for d in order_j:
        arrived(sgr.at[jat(-d)], (ss, sr), (d,))

    state = sgr[:, 0].reshape(width, width)
    grad = sgr[:, 1].reshape(width, width)
    y_mat = y_0 + mm(t_k, grad, NT)
    b_y = beta * y_mat
    ggs[2] = b_y.astype(BF16)

    def share(src, dst, m):
        for n, e in far_evens:
            push(src, dst, (gs, grs), (m, n), jdev(e))
        push(src, dst, (hs, hr), (m, 0), sibdev)

    def shared(at, m):
        for n, e in enumerate(evens):
            part = at(jat(-e))
            arrived(part, (gs, grs), (m, n))
            push(part, part, (hs, hr), (m, n + 1), sibdev)

    def collected(at, m):
        for n, e in enumerate([0] + evens):
            arrived(at(lax.rem(sib - e + nj, nj)), (hs, hr), (m, n))

    gg[j, 2] = ggs[2]
    share(ggs.at[2], gg.at[j, 2], 2)
    fresh = u_mat - mm(w_mat, state, NT)
    o_ref[...] = mm(q_eff, state, NT) + m_u
    stores = [pltpu.make_async_copy(o_ref, o_out, ls.at[5])]
    stores[0].start()
    d_m = jnp.where(lower_d, mm(cot, fresh, NT), 0.0)
    d_q = mm(cot, state) + mm(d_m, k)
    ggs[0] = (q_scale * (d_q - q * jnp.sum(d_q * q, axis=1, keepdims=True))).astype(BF16)
    gg[j, 0] = ggs[0]
    share(ggs.at[0], gg.at[j, 0], 0)
    rest = v - mm(k, state, NT)
    d_mt = jnp.where(upper_d, mm(fresh, cot, NT), 0.0)
    yd = jnp.where(lower, mm(y_mat, fresh, NT), 0.0)
    both = beta * yd + jnp.where(upper, mm(fresh, b_y, NT), 0.0)
    d_k = mm(fresh, grad) - mm(b_y, state) + mm(d_mt, q) - mm(both, k)
    ggs[1] = (k_scale * (d_k - k * jnp.sum(d_k * k, axis=1, keepdims=True))).astype(BF16)
    gg[j, 1] = ggs[1]
    share(ggs.at[1], gg.at[j, 1], 1)
    d_beta = jnp.sum(y_mat * rest - yd * gram, axis=1, keepdims=True)
    d_logit = d_beta * beta * (1.0 - 0.5 * beta)
    dl_row = jnp.sum(eye * d_logit, axis=0, keepdims=True)
    gbs[...] = jnp.broadcast_to(dl_row, (16, tok)).astype(BF16)
    gbr[j] = gbs[...]
    share(gbs, gbr.at[j], 3)

    for d in order_j:
        arrived(xr.at[jat(-d)], (xs, xrs), (d,))
    x_t = jnp.concatenate([xr[i] for i in range(nj)], axis=1)

    outs = {0: gq_ref, 1: gk_ref, 2: gv_ref}
    places = [
        lambda i: gg.at[i, 0],
        lambda i: gg.at[i, 1],
        lambda i: gg.at[i, 2],
        lambda i: gbr.at[i],
    ]
    def spread(m):
        collected(places[m], m)
        part = mm1(x_t, gg[:, m].reshape(nj * tok, width)).reshape(ny, rw, width)
        pr[m, y] = jnp.zeros((rw, width), BF16)
        ps[m] = part.astype(BF16)
        for d in far_y:
            push(ps.at[m, yat(d)], pr.at[m, y], (ps_, prs), (m, d), ydev(d))
        own = part[0]
        for t in range(1, ny):
            own = jnp.where(t == y, part[t], own)
        outs[m][...] = own

    for m in (2, 0, 1, 3):
        shared(places[m], m)
    for m in (2, 0, 1):
        spread(m)
    collected(places[3], 3)
    pb = mm1(jnp.concatenate([gbr[i] for i in range(nj)], axis=1), x_t, NT)
    for g in range(fb // 128):
        pbs[g] = pb[:8, g * 128:(g + 1) * 128]
    for d in far_y:
        push(pbs.at[yat(d) * rw // 128], pbr.at[y], (pbs_, pbrs), (d,), ydev(d))
    pbr[y] = pbs[y * rw // 128]

    def store(src, dst, at):
        stores.append(pltpu.make_async_copy(src, dst, ls.at[at]))
        stores[-1].start()

    out_refs = {0: gq_out, 1: gk_out, 2: gv_out}
    for m in (2, 0, 1):
        for d in order_y:
            arrived(pr.at[m, yat(-d)], (ps_, prs), (m, d))
        outs[m][...] += jnp.sum(pr[m].astype(F32), axis=0)
        store(outs[m], out_refs[m], 6 + m)
    for d in order_y:
        arrived(pbr.at[yat(-d)], (pbs_, pbrs), (d,))
    pb_row = jnp.sum(pbr[...], axis=0)[:1]
    gb_row = jnp.zeros((1, rw), F32)
    for g in range(per):
        gb_row = jnp.where(lax.rem(y, per) == g, pb_row[:, g * rw:(g + 1) * rw], gb_row)
    gb_ref[...] = gb_row
    store(gb_ref, gb_out, 9)

    drain()
    for copy in stores:
        copy.wait()


def write_out(o_in, gq_in, gk_in, gv_in, gb_in, o_out, gq_out, gk_out, gv_out, gb_out, sems):
    pairs = [(o_in, o_out), (gq_in, gq_out), (gk_in, gk_out), (gv_in, gv_out), (gb_in, gb_out)]
    copies = [pltpu.make_async_copy(pairs[i][0], pairs[i][1], sems.at[i]) for i in range(5)]
    for copy in copies:
        copy.start()
    for copy in copies:
        copy.wait()


def per_device(mesh, *args):
    inputs, w_query, w_key, w_value, w_beta, beta_bias, cotangent = args
    nz = mesh.shape["head"]
    ny = nz
    nj = mesh.shape["seq"] // ny
    tok, fb = inputs.shape
    rw, width = w_query.shape
    vp = width // nj
    ne = nj // 2
    vmem = pl.BlockSpec(memory_space=pltpu.VMEM)
    hbm = pl.BlockSpec(memory_space=pl.ANY)
    dma = pltpu.SemaphoreType.DMA
    scratch = [
        pltpu.VMEM((tok, width), F32),
        pltpu.VMEM((rw, width), F32),
        pltpu.VMEM((rw, width), F32),
        pltpu.VMEM((rw, width), F32),
        pltpu.VMEM((1, rw), F32),
        pltpu.VMEM((tok, width), F32),
        pltpu.VMEM((1, rw), BF16),
        pltpu.VMEM((nj, ny, rw, width), BF16),
        pltpu.VMEM((nj, ny, 2 * rw, width), BF16),
        pltpu.VMEM((ny, 16, 128), BF16),
        pltpu.VMEM((nj, 16, 128), BF16),
        pltpu.VMEM((nz, tok, fb), BF16),
        pltpu.VMEM((nj, nz * rw, tok), BF16),
        pltpu.VMEM((nj, nz * rw, tok), BF16),
        pltpu.VMEM((nj, width, width), F32),
        pltpu.VMEM((nj, 2, vp, width), F32),
        pltpu.VMEM((nj, 2, vp, width), F32),
        pltpu.VMEM((2, vp, width), F32),
        pltpu.VMEM((2, ny, width // 2, width), BF16),
        pltpu.VMEM((ny, vp, width), F32),
        pltpu.VMEM((nj, 2, vp, width), F32),
        pltpu.VMEM((nj, 2, vp, width), F32),
        pltpu.VMEM((3, tok, width), BF16),
        pltpu.VMEM((nj, 3, tok, width), BF16),
        pltpu.VMEM((16, tok), BF16),
        pltpu.VMEM((nj, 16, tok), BF16),
        pltpu.VMEM((3, ny, rw, width), BF16),
        pltpu.VMEM((3, ny, rw, width), BF16),
        pltpu.VMEM((fb // 128, 8, 128), F32),
        pltpu.VMEM((ny, 8, 128), F32),
        dma((11,)),
        dma((nz,)), dma((nz,)),
        dma((ny,)), dma((ny,)),
        dma((ne, ny)), dma((ne, ny)),
        dma((ne, ny)), dma((ne, ny)),
        dma((ny,)), dma((ny,)),
        dma((ne,)), dma((ne,)),
        dma((ne,)), dma((ne,)),
        dma((ny,)), dma((ny,)),
        dma((ne,)), dma((ne,)),
        dma((ne,)), dma((ne,)),
        dma((ne,)), dma((ne,)),
        dma((ne,)), dma((ne,)),
        dma((nj,)), dma((nj,)),
        dma((ny,)), dma((ny,)),
        dma((ny,)), dma((ny,)),
        dma((1,)), dma((1,)),
        dma((nj,)), dma((nj,)),
        dma((nj,)), dma((nj,)),
        dma((4, ne)), dma((4, ne)),
        dma((4, ne)), dma((4, ne)),
        dma((3, ny)), dma((3, ny)),
        dma((ny,)), dma((ny,)),
    ]
    results = pl.pallas_call(
        functools.partial(kernel, nz, ny, nj),
        out_shape=(
            jax.ShapeDtypeStruct((tok, width), F32),
            jax.ShapeDtypeStruct((rw, width), F32),
            jax.ShapeDtypeStruct((rw, width), F32),
            jax.ShapeDtypeStruct((rw, width), F32),
            jax.ShapeDtypeStruct((1, rw), F32),
        ),
        in_specs=[hbm, hbm, hbm, hbm, hbm, pl.BlockSpec(memory_space=pltpu.SMEM), hbm],
        out_specs=(hbm,) * 5,
        scratch_shapes=scratch,
        compiler_params=pltpu.CompilerParams(
            collective_id=0, has_side_effects=True, vmem_limit_bytes=60 * 1024 * 1024
        ),
        name="delta_step",
    )(inputs, w_query, w_key, w_value, w_beta.reshape(1, rw), beta_bias, cotangent)
    results = pl.pallas_call(
        write_out,
        out_shape=[jax.ShapeDtypeStruct(r.shape, F32) for r in results],
        in_specs=[vmem] * 5,
        out_specs=[hbm] * 5,
        scratch_shapes=[dma((5,))],
        name="write_out",
    )(*results)
    return (results[0], results[1], results[2], results[3], results[4].reshape(rw, 1))


def solution(mesh):
    return jax.shard_map(
        functools.partial(per_device, mesh),
        mesh=mesh,
        in_specs=(P("seq", "head"),) * 5 + (P("head"), P("seq", "head")),
        out_specs=(P("seq", "head"),) * 5,
        check_vma=False,
    )
```
